32 devices in a mesh: dp: 2 (over core), seq: 2 (over x), vocab: 8 (over z, y).
Axes of the slice: x: 2, y: 2, z: 4, core: 2. Of those that a mesh axis runs over, the one named last changes fastest.
Arguments:
- hidden_states: bfloat16 [6, 256, 4096], P('dp', 'seq', 'vocab'), may hold values from -6 to 6
- head_weight: bfloat16 [4096, 32000], P('seq', 'vocab'), may hold values from -0.09375 to 0.09375
- owner_pos: int32 [6, 32000], P('dp', 'vocab'), may hold values from 0 to 255
- token_ids: int32 [6, 256], P('dp', 'seq'), may hold values from 0 to 31999, as said below
- teacher_margin: float32 [2], P('dp'), may hold values from -150 to 150
Outputs:
- grad_head: float32 [4096, 32000], P('seq', 'vocab')
- grad_hidden: bfloat16 [6, 256, 4096], P('dp', 'seq', 'vocab')
The draws below stay inside these ranges and needn't reach their ends.
Inputs may be any that keep to these rules, and one draw needn't show every extreme that they name: `owner_pos`: owner positions may fall on padding tokens, which then pool nothing. `token_ids`: 0 marks padding, which fills a tail of one or more positions of every document; a document's first token is 31999.
All inputs are finite; a program needn't handle non-finite values.
Results may differ from the reference program's by a relative error of at most 0.017.
Values may be sent and summed in bfloat16 or wider, within the bound.
No kernel may reach another device: no remote copies, remote signals or barrier semaphores. Data moves between devices by JAX's collectives and lax.ppermute only.
A program may use at most 256 MiB of HBM per device.

```python
import jax
import jax.numpy as jnp
from jax import lax

D = 4096
VOCAB = 32000
TRIPLES = 2
DOCS = 6
L = 256
N_VOCAB = 8


def draw_token_ids(key, part):
    key_length, key_values = jax.random.split(key)
    lengths = jax.random.randint(key_length, (DOCS, 1), L // 2, L)
    values = jax.random.randint(key_values, (DOCS, L), 1, VOCAB)
    positions = jnp.arange(L, dtype=jnp.int32)[None, :]
    values = jnp.where(positions < lengths, values, 0)
    values = values.at[:, 0].set(VOCAB - 1)
    return values.astype(jnp.int32)


def plant(values, stream_key, least, top_value):
    extent = values.shape
    place = [jax.random.randint(jax.random.fold_in(stream_key, axis), (), 0, extent[axis]) for axis in range(len(extent))]
    values = values.at[tuple(place)].set(least)
    longest = extent.index(max(extent))
    place[longest] = (place[longest] + 1) % extent[longest]
    return values.at[tuple(place)].set(top_value)


def shard_levels(stream_key, dims, cuts, low, high):
    factor_of, own = 1.0, jax.random.fold_in(stream_key, 6)
    for position, parts in cuts:
        draws = jnp.exp(jax.random.uniform(jax.random.fold_in(own, position), (parts,), jnp.float32, low / len(cuts), high / len(cuts)))
        factor_of = factor_of * jnp.repeat(draws, dims[position] // parts).reshape([-1 if axis == position else 1 for axis in range(len(dims))])
    return factor_of


def scatter_about(key, dims, width, limit, cuts=(), kind=jnp.bfloat16):
    level = shard_levels(key, dims, cuts, -0.22, 0.18) if cuts else 1.0
    result = jax.random.normal(key, dims, jnp.float32) * width * level
    return jnp.minimum(jnp.maximum(result, -limit), limit).astype(kind)


def setup_inputs(seed: int = 0) -> dict:
    arg_keys = jax.random.split(jax.random.key(seed), 6)
    return {
        "hidden_states": scatter_about(arg_keys[0], (DOCS, L, D), 1.0, 6.0, ((0, 2), (1, 2), (2, 8))),
        "head_weight": scatter_about(arg_keys[1], (D, VOCAB), D ** -0.5, 0.09375, ((0, 2), (1, 8))),
        "owner_pos": plant(jax.random.randint(arg_keys[2], (DOCS, VOCAB), 0, L), jax.random.fold_in(arg_keys[2], 1), 0, L - 1).astype(jnp.int32),
        "token_ids": draw_token_ids(jax.random.fold_in(arg_keys[5], 71), 0),
        "teacher_margin": scatter_about(arg_keys[4], (TRIPLES,), 30.0, 150.0, ((0, 2),), jnp.float32),
    }


def pick_rows(features, places):
    return features[places]

def reference(hidden_states, head_weight, owner_pos, token_ids, teacher_margin):
    block_count = N_VOCAB
    block_size = VOCAB // block_count
    head_blocks = head_weight.T.reshape(block_count, block_size, D)

    def doc_logits(inputs):
        features, places = inputs

        def block_logits(pair):
            block_places, block_head = pair
            owner_rows = pick_rows(features, block_places).astype(jnp.float32)
            return lax.optimization_barrier(jnp.sum(owner_rows * block_head.astype(jnp.float32), axis=1))
        return lax.map(block_logits, (places.reshape(block_count, block_size), head_blocks)).reshape(VOCAB)
    logits = lax.map(doc_logits, (hidden_states, owner_pos))
    validity = (jnp.take_along_axis(token_ids, owner_pos, axis=1) != 0).astype(jnp.float32)
    softened = jax.nn.softplus(logits)
    pooled = validity * jnp.log1p(softened)
    slopes = validity * jax.nn.sigmoid(logits) / (1.0 + softened)
    triple_view = pooled.reshape(TRIPLES, 3, VOCAB)
    positive = lax.optimization_barrier(jnp.sum(triple_view[:, 0] * triple_view[:, 1], axis=1))
    negative = lax.optimization_barrier(jnp.sum(triple_view[:, 0] * triple_view[:, 2], axis=1))
    margin_grad = (positive - negative - teacher_margin) / TRIPLES
    scale = margin_grad[:, None]
    pooled_grad = jnp.stack([scale * (triple_view[:, 1] - triple_view[:, 2]), scale * triple_view[:, 0], -scale * triple_view[:, 0]], axis=1).reshape(DOCS, VOCAB)
    grad_logit = (pooled_grad * slopes).astype(jnp.bfloat16)

    def head_block(inputs):
        block_places, block_grads = inputs
        owner_rows = jax.vmap(pick_rows)(hidden_states, block_places).astype(jnp.float32)
        return jnp.einsum('kvd,kv->dv', owner_rows, block_grads.astype(jnp.float32), precision=lax.Precision.HIGHEST)
    places_blocks = owner_pos.reshape(DOCS, block_count, block_size).transpose(1, 0, 2)
    grads_blocks = grad_logit.reshape(DOCS, block_count, block_size).transpose(1, 0, 2)
    head_parts = lax.map(head_block, (places_blocks, grads_blocks))
    grad_head = head_parts.transpose(1, 0, 2).reshape(D, VOCAB)

    def doc_grad(inputs):
        places, grads = inputs

        def advance(running, block):
            block_places, block_grads, block_head = block
            products = block_grads.astype(jnp.float32)[:, None] * block_head.astype(jnp.float32)
            partial_value = jax.ops.segment_sum(products, block_places, num_segments=L)
            rounded = lax.optimization_barrier(partial_value.astype(jnp.bfloat16))
            return (running + rounded.astype(jnp.float32), None)
        running, _ = lax.scan(advance, jnp.zeros((L, D), jnp.float32), (places.reshape(block_count, block_size), grads.reshape(block_count, block_size), head_blocks))
        return running.astype(jnp.bfloat16)
    grad_hidden = lax.map(doc_grad, (owner_pos, grad_logit))
    return (grad_head, grad_hidden)
```

```python
import functools

import jax
import jax.numpy as jnp
from jax import lax
from jax.experimental import pallas as pl
from jax.experimental.pallas import tpu as pltpu
from jax.sharding import PartitionSpec as P

LANES = 128
VMEM_BYTES = 24 * 1024 * 1024


def shift_perm(count, shift):
    return [(i, (i + shift) % count) for i in range(count)]


def divisor(terms, limit):
    fits = [b for b in range(16, limit + 1, 16) if terms % b == 0]
    return fits[-1] if fits else terms


def ring_place(z, count):
    return jnp.where(z % 2 == 1, (z + 1) // 2, jnp.where(z == 0, 0, count - z // 2))


def ring_member(place, count):
    return jnp.where(place == 0, 0, jnp.where(place <= count // 2, 2 * place - 1, 2 * (count - place)))


def logits_kernel(docs, inner, strips, *refs):
    index_ref = refs[0]
    pieces = refs[1:1 + inner]
    heads = refs[1 + inner:1 + inner + strips]
    places_ref, logits_ref, rows_ref = refs[1 + inner + strips:]
    slots, near, _, part, width = pieces[0].shape
    length = slots * part

    @pl.when(pl.program_id(0) == 0)
    def _():
        for q in range(inner):
            lane_y = lax.rem(index_ref[0] + q, inner)
            for n in range(near):
                lane = pl.multiple_of((n * inner + lane_y) * width, width)
                for k in range(docs):
                    for s in range(slots):
                        rows_ref[pl.ds(k * length + s * part, part), pl.ds(lane, width)] = pieces[q][s, n, k]

    head = jnp.concatenate([ref[...] for ref in heads], axis=1)
    token = lax.broadcasted_iota(jnp.int32, (length, head.shape[0]), 0)
    for k in range(docs):
        dense = lax.dot_general(
            rows_ref[pl.ds(k * length, length), :],
            head,
            (((1,), (1,)), ((), ())),
            preferred_element_type=jnp.float32,
        )
        picked = jnp.where(token == places_ref[pl.ds(k, 1), :], dense, 0.0)
        logits_ref[pl.ds(k, 1), :] = jnp.sum(picked, axis=0, keepdims=True)


def hidden_kernel(docs, inner, strips, shape, *refs):
    index_ref = refs[0]
    heads = refs[1:1 + strips]
    places_ref, grads_ref = refs[1 + strips:3 + strips]
    outs = refs[3 + strips:3 + strips + inner]
    total_ref = refs[-1]
    slots, near, _, part, width = shape
    length = slots * part
    step = pl.program_id(0)
    head = jnp.concatenate([ref[...] for ref in heads], axis=1)
    token = lax.broadcasted_iota(jnp.int32, (length, head.shape[0]), 0)

    @pl.when(step == 0)
    def _():
        total_ref[...] = jnp.zeros_like(total_ref)

    for k in range(docs):
        spread = jnp.where(token == places_ref[pl.ds(k, 1), :], grads_ref[pl.ds(k, 1), :], 0.0)
        total_ref[pl.ds(k * length, length), :] += jnp.dot(
            spread.astype(jnp.bfloat16), head, preferred_element_type=jnp.float32
        )

    @pl.when(step == pl.num_programs(0) - 1)
    def _():
        for q in range(inner):
            lane_y = lax.rem(index_ref[0] + q, inner)
            for n in range(near):
                lane = pl.multiple_of((n * inner + lane_y) * width, width)
                for k in range(docs):
                    for s in range(slots):
                        piece = total_ref[pl.ds(k * length + s * part, part), pl.ds(lane, width)]
                        outs[q][s, n, k] = piece.astype(jnp.bfloat16)


def head_kernel(groups, docs, *refs):
    index_ref = refs[0]
    rows = refs[1:1 + groups]
    columns_ref = refs[1 + groups]
    out_ref, spread_ref = refs[-2:]
    tokens = rows[0].shape[0]
    length = tokens // docs
    count = groups * docs

    @pl.when(pl.program_id(0) == 0)
    def _():
        token = lax.broadcasted_iota(jnp.int32, (out_ref.shape[0], length), 1).astype(jnp.float32)
        for k in range(count):
            spread = jnp.where(token == columns_ref[:, k:k + 1], columns_ref[:, count + k:count + k + 1], 0.0)
            spread_ref[:, k * length:(k + 1) * length] = spread.astype(jnp.bfloat16)

    total = None
    for g in range(groups):
        features = rows[0][...]
        for j in range(1, groups):
            features = jnp.where(lax.rem(index_ref[1] + j, groups) == g, rows[j][...], features)
        term = jnp.dot(
            spread_ref[:, g * tokens:(g + 1) * tokens], features, preferred_element_type=jnp.float32
        )
        total = term if total is None else total + term
    out_ref[...] = total


def on_device(axes, hidden_states, head_weight, owner_pos, token_ids, teacher_margin):
    groups, slots, blocks = axes
    docs, part, block_width = hidden_states.shape
    depth, terms = head_weight.shape
    triples = teacher_margin.shape[0]
    inner = 2 if blocks % 2 == 0 else 1
    outer = blocks // inner
    near = outer // slots
    chunks = max(1, block_width // LANES)
    width = block_width // chunks
    length = slots * part
    tokens = docs * length
    columns = divisor(terms, 2048)
    steps = terms // columns
    strips = near * inner

    group = lax.axis_index("dp")
    seq = lax.axis_index("seq")
    block = lax.axis_index("vocab")
    block_y = lax.rem(block, inner)
    place = ring_place(lax.div(block, inner), outer)
    order = [0] + list(range(1, outer, 2)) + [z for z in range(outer - 1, 0, -1) if z % 2 == 0]
    ring = [
        (order[p] * inner + y, order[(p + 1) % outer] * inner + y) for p in range(outer) for y in range(inner)
    ]
    index = jnp.stack([block_y, group]).astype(jnp.int32)

    def across_y(value, shift):
        perm = [(z * inner + y, z * inner + (y + shift) % inner) for z in range(outer) for y in range(inner)]
        return lax.ppermute(value, "vocab", perm)

    def other_groups(value):
        return [value] + [lax.ppermute(value, "dp", shift_perm(groups, -g)) for g in range(1, groups)]

    def in_group_order(values):
        doubled = jnp.stack(values + values)
        return lax.dynamic_slice_in_dim(doubled, lax.rem(groups - group, groups), groups, axis=0)

    def blocked(value):
        return value.reshape(docs, steps, columns).transpose(1, 0, 2)

    head_rows = head_weight.T
    strip_specs = lambda c: [
        pl.BlockSpec((columns, width), functools.partial(lambda lane, v: (v, lane), strip * chunks + c))
        for strip in range(strips)
    ]
    row_spec = pl.BlockSpec((pl.squeezed, docs, columns), lambda v: (v, 0, 0))
    piece_shape = (slots, near, docs, part, width)
    piece_spec = pl.BlockSpec(piece_shape, lambda v: (0, 0, 0, 0, 0))
    index_spec = pl.BlockSpec(memory_space=pltpu.SMEM)
    params = pltpu.CompilerParams(vmem_limit_bytes=VMEM_BYTES)

    owner_blocks = blocked(owner_pos)
    places = lax.rem(owner_blocks + (length - seq * part), length)
    own_lengths = jnp.sum((token_ids != 0).astype(jnp.int32), axis=1, keepdims=True)
    lengths = own_lengths
    for s in range(1, slots):
        lengths = lengths + lax.ppermute(own_lengths, "seq", shift_perm(slots, s))
    validity = (owner_blocks < lengths[None]).astype(jnp.float32)
    places_all = in_group_order(other_groups(places))

    logit_parts = []
    feature_parts = []
    for c in range(chunks):
        held = [hidden_states[:, :, c * width:(c + 1) * width]]
        for _ in range(outer - 1):
            held.append(lax.ppermute(held[-1], "vocab", ring))
        held = jnp.stack(held)

        def of_half(half):
            picks = [
                lax.dynamic_index_in_dim(
                    held, lax.rem(place + outer - ring_place(half * near + n, outer), outer), 0, keepdims=False
                )
                for n in range(near)
            ]
            return jnp.stack(picks)

        gathered = [of_half(seq)]
        for s in range(1, slots):
            gathered.append(lax.ppermute(of_half(lax.rem(seq + slots - s, slots)), "seq", shift_perm(slots, -s)))
        gathered = jnp.stack(gathered)
        pieces = [gathered] + [across_y(gathered, -q) for q in range(1, inner)]
        chunk_logits, chunk_features = pl.pallas_call(
            functools.partial(logits_kernel, docs, inner, strips),
            grid=(steps,),
            in_specs=[index_spec] + [piece_spec] * inner + strip_specs(c) + [row_spec],
            out_specs=[row_spec, pl.BlockSpec((tokens, strips * width), lambda v: (0, 0))],
            out_shape=[
                jax.ShapeDtypeStruct((steps, docs, columns), jnp.float32),
                jax.ShapeDtypeStruct((tokens, strips * width), jnp.bfloat16),
            ],
            compiler_params=params,
            cost_estimate=pl.CostEstimate(
                flops=2 * tokens * strips * width * terms,
                bytes_accessed=2 * strips * width * (terms + 2 * tokens),
                transcendentals=0,
            ),
            name="pooled_logits",
        )(index, *pieces, *[head_rows] * strips, places)
        logit_parts.append(chunk_logits)
        feature_parts.append(chunk_features)

    logit_part = functools.reduce(jnp.add, logit_parts)
    logits = logit_part
    for s in range(1, slots):
        logits = logits + lax.ppermute(logit_part, "seq", shift_perm(slots, s))
    softened = jax.nn.softplus(logits)
    pooled = validity * jnp.log1p(softened)
    slopes = validity * jax.nn.sigmoid(logits) / (1.0 + softened)
    view = pooled.reshape(steps, triples, 3, columns)
    query, positive, negative = view[:, :, 0], view[:, :, 1], view[:, :, 2]
    unscaled = jnp.stack([positive - negative, query, -query], axis=2).reshape(logits.shape) * slopes
    unscaled = unscaled.astype(jnp.bfloat16).astype(jnp.float32)
    scores = jnp.sum(query * positive, axis=(0, 2)) - jnp.sum(query * negative, axis=(0, 2))
    if blocks & (blocks - 1) == 0:
        distance = 1
        while distance < blocks:
            scores = scores + lax.ppermute(scores, "vocab", [(i, i ^ distance) for i in range(blocks)])
            distance *= 2
    else:
        scores = lax.psum(scores, "vocab")
    margin = (scores - teacher_margin) / (triples * groups)
    factors = jnp.repeat(margin, 3)
    scaled = (unscaled * factors[:, None]).astype(jnp.bfloat16)
    scaled_all = in_group_order(other_groups(scaled)).astype(jnp.float32)
    head_columns = jnp.concatenate([places_all.astype(jnp.float32), scaled_all])
    head_columns = head_columns.transpose(1, 3, 0, 2).reshape(terms, 2 * groups * docs)
    features = jnp.stack([part.reshape(tokens, strips, width) for part in feature_parts], axis=2)
    features_all = other_groups(features.reshape(tokens, depth))

    hidden_parts = []
    for c in range(chunks):
        parts = pl.pallas_call(
            functools.partial(hidden_kernel, docs, inner, strips, piece_shape),
            grid=(steps,),
            in_specs=[index_spec] + strip_specs(c) + [row_spec, row_spec],
            out_specs=[piece_spec] * inner,
            out_shape=[jax.ShapeDtypeStruct(piece_shape, jnp.bfloat16)] * inner,
            scratch_shapes=[pltpu.VMEM((tokens, strips * width), jnp.float32)],
            compiler_params=params,
            cost_estimate=pl.CostEstimate(
                flops=2 * tokens * strips * width * terms,
                bytes_accessed=2 * strips * width * (terms + tokens),
                transcendentals=0,
            ),
            name="hidden_terms",
        )(index, *[head_rows] * strips, places, unscaled)
        total = parts[0].astype(jnp.float32)
        for q in range(1, inner):
            total = total + across_y(parts[q], q).astype(jnp.float32)
        total = total.astype(jnp.bfloat16)
        mine = [total[0]]
        for s in range(1, slots):
            mine.append(lax.ppermute(total[s], "seq", shift_perm(slots, s)))
        mine = jnp.concatenate(mine)

        def piece_at(back):
            z = ring_member(lax.rem(place + outer - back, outer), outer)
            slot = lax.rem(seq + slots - lax.div(z, near), slots)
            return lax.dynamic_index_in_dim(mine, slot * near + lax.rem(z, near), 0, keepdims=False)

        running = piece_at(1)
        for back in range(2, outer + 1):
            arrived = lax.ppermute(running, "vocab", ring).astype(jnp.float32)
            running = arrived + piece_at(back).astype(jnp.float32)
            if back < outer:
                running = running.astype(jnp.bfloat16)
        hidden_parts.append((running * factors[:, None, None]).astype(jnp.bfloat16))
    grad_hidden = jnp.concatenate(hidden_parts, axis=2)

    head_terms = divisor(terms, 1024)
    lane_block = min(depth, 512)
    grad_head = None
    for r in range(terms // head_terms):
        previous = [] if grad_head is None else [grad_head]
        grad_head = pl.pallas_call(
            functools.partial(head_kernel, groups, docs),
            grid=(depth // lane_block,),
            in_specs=[index_spec]
            + [pl.BlockSpec((tokens, lane_block), lambda d: (0, d))] * groups
            + [pl.BlockSpec((head_terms, 2 * groups * docs), functools.partial(lambda r, d: (r, 0), r))]
            + [pl.BlockSpec(memory_space=pl.ANY)] * len(previous),
            out_specs=pl.BlockSpec((head_terms, lane_block), functools.partial(lambda r, d: (r, d), r)),
            out_shape=jax.ShapeDtypeStruct((terms, depth), jnp.float32),
            scratch_shapes=[pltpu.VMEM((head_terms, groups * tokens), jnp.bfloat16)],
            input_output_aliases={2 + groups: 0} if previous else {},
            compiler_params=params,
            cost_estimate=pl.CostEstimate(
                flops=2 * groups * tokens * head_terms * depth,
                bytes_accessed=4 * head_terms * depth + 2 * groups * tokens * depth,
                transcendentals=0,
            ),
            name="head_terms",
        )(index, *features_all, head_columns, *previous)
    return (grad_head.T, grad_hidden)


def solution(mesh):
    axes = (mesh.shape["dp"], mesh.shape["seq"], mesh.shape["vocab"])
    return jax.shard_map(
        functools.partial(on_device, axes),
        mesh=mesh,
        in_specs=(
            P("dp", "seq", "vocab"),
            P("seq", "vocab"),
            P("dp", "vocab"),
            P("dp", "seq"),
            P("dp"),
        ),
        out_specs=(P("seq", "vocab"), P("dp", "seq", "vocab")),
        check_vma=False,
    )
```

```python
import functools

import jax
import jax.numpy as jnp
from jax import lax
from jax.experimental import pallas as pl
from jax.experimental.pallas import tpu as pltpu
from jax.sharding import PartitionSpec as P

LANES = 128
VMEM_BYTES = 48 * 1024 * 1024


def shift_perm(count, shift):
    return [(i, (i + shift) % count) for i in range(count)]


def waiting(kernel, count):
    return lambda *refs: kernel(refs[0], *refs[1 + count:])


def divisor(terms, limit):
    fits = [b for b in range(16, limit + 1, 16) if terms % b == 0]
    return fits[-1] if fits else terms


def slice_kernel(index_ref, states_ref, out_ref):
    out_ref[...] = states_ref[...]


def pick_kernel(slots, near, outer, index_ref, *refs):
    held = refs[:outer]
    gathered_ref = refs[outer]
    sends = refs[outer + 1:]
    block_z, seq = index_ref[2], index_ref[3]
    for s in range(slots):
        target = gathered_ref.at[0] if s == 0 else sends[s - 1]
        half = lax.rem(seq + slots - s, slots)
        for n in range(near):
            back = lax.rem(block_z + outer - (half * near + n), outer)
            for b in range(outer):

                @pl.when(back == b)
                def _():
                    target[n] = held[b][...]


def logits_kernel(docs, inner, strips, *refs):
    index_ref = refs[0]
    pieces = refs[1:1 + inner]
    heads = refs[1 + inner:1 + inner + strips]
    places_ref = refs[1 + inner + strips]
    logits_ref, rows_ref = refs[-2:]
    slots, near, _, part, width = pieces[0].shape
    length = slots * part

    @pl.when(pl.program_id(0) == 0)
    def _():
        for q in range(inner):
            lane_y = lax.rem(index_ref[0] + q, inner)
            for n in range(near):
                lane = pl.multiple_of((n * inner + lane_y) * width, width)
                for k in range(docs):
                    for s in range(slots):
                        rows_ref[pl.ds(k * length + s * part, part), pl.ds(lane, width)] = pieces[q][s, n, k]

    head = jnp.concatenate([ref[...] for ref in heads], axis=1)
    dense = lax.dot_general(
        rows_ref[...], head, (((1,), (1,)), ((), ())), preferred_element_type=jnp.float32
    )
    token = lax.broadcasted_iota(jnp.int32, (length, head.shape[0]), 0)
    for k in range(docs):
        picked = jnp.where(token == places_ref[pl.ds(k, 1), :], dense[k * length:(k + 1) * length], 0.0)
        logits_ref[pl.ds(k, 1), :] = jnp.sum(picked, axis=0, keepdims=True)


def hidden_kernel(docs, inner, strips, shape, *refs):
    index_ref = refs[0]
    heads = refs[1:1 + strips]
    places_ref, grads_ref = refs[1 + strips:3 + strips]
    outs = refs[3 + strips:3 + strips + inner]
    spread_ref, total_ref = refs[-2:]
    slots, near, _, part, width = shape
    length = slots * part
    step = pl.program_id(0)
    head = jnp.concatenate([ref[...] for ref in heads], axis=1)
    token = lax.broadcasted_iota(jnp.int32, (length, head.shape[0]), 0)
    for k in range(docs):
        spread = jnp.where(token == places_ref[pl.ds(k, 1), :], grads_ref[pl.ds(k, 1), :], 0.0)
        spread_ref[pl.ds(k * length, length), :] = spread.astype(jnp.bfloat16)
    term = jnp.dot(spread_ref[...], head, preferred_element_type=jnp.float32)

    @pl.when(step == 0)
    def _():
        total_ref[...] = term

    @pl.when(step > 0)
    def _():
        total_ref[...] += term

    @pl.when(step == pl.num_programs(0) - 1)
    def _():
        for q in range(inner):
            lane_y = lax.rem(index_ref[0] + q, inner)
            for n in range(near):
                lane = pl.multiple_of((n * inner + lane_y) * width, width)
                for k in range(docs):
                    for s in range(slots):
                        piece = total_ref[pl.ds(k * length + s * part, part), pl.ds(lane, width)]
                        outs[q][s, n, k] = piece.astype(jnp.bfloat16)


def combine_kernel(count, inner, slots, index_ref, *refs):
    outs = refs[count * inner:]
    for i in range(count):
        parts = refs[i * inner:(i + 1) * inner]
        for s in range(slots):
            total = parts[0][s].astype(jnp.float32)
            for other in parts[1:]:
                total = total + other[s].astype(jnp.float32)
            outs[s][i] = total.astype(jnp.bfloat16)


def sort_kernel(slots, near, outer, index_ref, *refs):
    mine, outs = refs[:slots], refs[slots:]
    block_z, seq = index_ref[2], index_ref[3]
    for ahead in range(outer):
        z = lax.rem(block_z + ahead, outer)
        slot = lax.rem(seq + slots - lax.div(z, near), slots)
        for s in range(slots):

            @pl.when(slot == s)
            def _():
                outs[ahead][...] = mine[s][:, lax.rem(z, near)]


def finish_kernel(counts, outer, index_ref, margin_ref, *refs):
    out_ref = refs[-1]
    docs = out_ref.shape[0]
    width = refs[0].shape[-1]
    c = 0
    for group, count in enumerate(counts):
        arrived = refs[group * outer:(group + 1) * outer]
        for i in range(count):
            for k in range(docs):
                total = arrived[0][i, k].astype(jnp.float32)
                for other in arrived[1:]:
                    total = total + other[i, k].astype(jnp.float32)
                out_ref[k, :, c * width:(c + 1) * width] = (total * margin_ref[k // 3]).astype(jnp.bfloat16)
            c += 1


def head_kernel(groups, docs, *refs):
    index_ref, margin_ref = refs[:2]
    rows = refs[2:2 + groups]
    places_ref, grads_ref = refs[2 + groups:4 + groups]
    out_ref, token_ref, spread_ref = refs[-3:]
    chunks, tokens, width = rows[0].shape
    length = tokens // docs

    @pl.when(pl.program_id(1) == 0)
    def _():
        token_ref[...] = jnp.zeros_like(token_ref)
        token = lax.broadcasted_iota(jnp.int32, (out_ref.shape[0], length), 1)
        for k in range(groups * docs):
            grads = grads_ref[:, k:k + 1] * margin_ref[k // 3]
            spread = jnp.where(token == places_ref[:, k:k + 1], grads, 0.0)
            spread_ref[:, k * length:(k + 1) * length] = spread.astype(jnp.bfloat16)

    for first in range(groups):

        @pl.when(index_ref[1] == first)
        def _():
            total = None
            for g in range(groups):
                ref = rows[(g - first) % groups]
                features = jnp.concatenate([ref[c] for c in range(chunks)], axis=1)
                term = jnp.dot(
                    spread_ref[:, g * tokens:(g + 1) * tokens], features, preferred_element_type=jnp.float32
                )
                total = term if total is None else total + term
            out_ref[...] = total


def on_device(axes, hidden_states, head_weight, owner_pos, token_ids, teacher_margin):
    groups, slots, blocks = axes
    docs, part, block_width = hidden_states.shape
    depth, terms = head_weight.shape
    triples = teacher_margin.shape[0]
    inner = 2 if blocks % 2 == 0 else 1
    outer = blocks // inner
    near = outer // slots
    chunks = max(1, block_width // LANES)
    width = block_width // chunks
    length = slots * part
    tokens = docs * length
    columns = divisor(terms, 2048)
    steps = terms // columns
    strips = near * inner

    group = lax.axis_index("dp")
    seq = lax.axis_index("seq")
    block = lax.axis_index("vocab")
    block_y = lax.rem(block, inner)
    block_z = lax.div(block, inner)
    index = jnp.stack([block_y, group, block_z, seq]).astype(jnp.int32)

    def across_y(value, shift):
        perm = [(z * inner + y, z * inner + (y + shift) % inner) for z in range(outer) for y in range(inner)]
        return lax.ppermute(value, "vocab", perm)

    def across_z(value, shift):
        perm = [(z * inner + y, (z + shift) % outer * inner + y) for z in range(outer) for y in range(inner)]
        return lax.ppermute(value, "vocab", perm)

    def other_groups(value):
        return [value] + [lax.ppermute(value, "dp", shift_perm(groups, -g)) for g in range(1, groups)]

    def in_group_order(values):
        doubled = jnp.stack(values + values)
        return lax.dynamic_slice_in_dim(doubled, lax.rem(groups - group, groups), groups, axis=0)

    def by_term(value):
        return value.transpose(1, 3, 0, 2).reshape(terms, groups * docs)

    def blocked(value):
        return value.reshape(docs, steps, columns).transpose(1, 0, 2)

    head_rows = head_weight.T
    strip_specs = lambda c: [
        pl.BlockSpec((columns, width), functools.partial(lambda lane, v: (v, lane), strip * chunks + c))
        for strip in range(strips)
    ]
    row_spec = pl.BlockSpec((pl.squeezed, docs, columns), lambda v: (v, 0, 0))
    piece_shape = (slots, near, docs, part, width)
    piece_spec = pl.BlockSpec(piece_shape, lambda v: (0, 0, 0, 0, 0))
    index_spec = pl.BlockSpec(memory_space=pltpu.SMEM)
    vmem_spec = pl.BlockSpec(memory_space=pltpu.VMEM)
    any_spec = pl.BlockSpec(memory_space=pl.ANY)
    params = pltpu.CompilerParams(vmem_limit_bytes=VMEM_BYTES)

    def cost(flops, transferred):
        return pl.CostEstimate(flops=int(flops), bytes_accessed=int(transferred), transcendentals=0)

    owner_blocks = blocked(owner_pos)
    places = lax.rem(owner_blocks + (length - seq * part), length)
    own_lengths = jnp.sum((token_ids != 0).astype(jnp.int32), axis=1, keepdims=True)
    lengths = own_lengths
    for s in range(1, slots):
        lengths = lengths + lax.ppermute(own_lengths, "seq", shift_perm(slots, s))
    validity = (owner_blocks < lengths[None]).astype(jnp.float32)
    places_all = by_term(in_group_order(other_groups(places)))

    def run(kernel, name, operands, specs, shapes, out_specs=None, waits=(), flops=0, aliases={}, scratch=(), grid=()):
        waits = [value for value in waits if value is not None]
        return pl.pallas_call(
            waiting(kernel, len(waits)),
            grid=grid,
            in_specs=[index_spec] + [any_spec] * len(waits) + specs,
            out_specs=out_specs or [vmem_spec] * len(shapes),
            out_shape=shapes,
            scratch_shapes=list(scratch),
            input_output_aliases={1 + len(waits) + i: o for i, o in aliases.items()},
            compiler_params=params,
            cost_estimate=cost(flops, flops // 64),
            name=name,
        )(index, *waits, *operands)

    bf16 = lambda *shape: jax.ShapeDtypeStruct(shape, jnp.bfloat16)
    moved_shape = bf16(near, docs, part, width)
    gathered_chunks = []
    others = []
    sent = None
    for c in range(chunks):
        (own,) = run(
            slice_kernel,
            "feature_chunk",
            [hidden_states],
            [pl.BlockSpec((docs, part, width), functools.partial(lambda c, i: (0, 0, c), c))],
            [bf16(docs, part, width)],
            out_specs=[pl.BlockSpec((docs, part, width), lambda i: (0, 0, 0))],
            waits=[sent],
            grid=(1,),
        )
        held = [own] + [across_z(own, back) for back in range(1, outer)]
        gathered, *sends = run(
            functools.partial(pick_kernel, slots, near, outer),
            "pick_halves",
            held,
            [vmem_spec] * outer,
            [bf16(*piece_shape)] + [moved_shape] * (slots - 1),
            waits=[gathered_chunks[c - 1] if c > 0 else None, others[c - 2] if c > 1 else None],
        )
        sent = gathered
        if slots > 1:
            arrived = [lax.ppermute(sends[s - 1], "seq", shift_perm(slots, -s)) for s in range(1, slots)]
            gathered = jnp.concatenate([gathered[:1]] + [value[None] for value in arrived])
        gathered_chunks.append(gathered)
        others.append(across_y(gathered, -1) if inner > 1 else None)

    logit_parts = []
    features = None
    for c in range(chunks):
        pieces = [gathered_chunks[c], others[c]][:inner]
        previous = [] if features is None else [features]
        chunk_logits, features = run(
            functools.partial(logits_kernel, docs, inner, strips),
            "pooled_logits",
            [*pieces, *[head_rows] * strips, places, *previous],
            [piece_spec] * inner + strip_specs(c) + [row_spec] + [any_spec] * len(previous),
            [
                jax.ShapeDtypeStruct((steps, docs, columns), jnp.float32),
                bf16(chunks, tokens, strips * width),
            ],
            out_specs=[
                row_spec,
                pl.BlockSpec(
                    (pl.squeezed, tokens, strips * width), functools.partial(lambda c, v: (c, 0, 0), c)
                ),
            ],
            waits=[None if previous else places_all],
            flops=2 * tokens * strips * width * terms,
            aliases={inner + strips + 1: 1} if previous else {},
            grid=(steps,),
        )
        logit_parts.append(chunk_logits)

    logit_part = functools.reduce(jnp.add, logit_parts)
    logits = logit_part
    for s in range(1, slots):
        logits = logits + lax.ppermute(logit_part, "seq", shift_perm(slots, s))
    softened = jax.nn.softplus(logits)
    pooled = validity * jnp.log1p(softened)
    slopes = validity * jax.nn.sigmoid(logits) / (1.0 + softened)
    view = pooled.reshape(steps, triples, 3, columns)
    query, positive, negative = view[:, :, 0], view[:, :, 1], view[:, :, 2]
    unscaled = jnp.stack([positive - negative, query, -query], axis=2).reshape(logits.shape) * slopes
    unscaled = unscaled.astype(jnp.bfloat16)
    scores = jnp.sum(query * positive, axis=(0, 2)) - jnp.sum(query * negative, axis=(0, 2))
    if blocks & (blocks - 1) == 0:
        distance = 1
        while distance < blocks:
            scores = scores + lax.ppermute(scores, "vocab", [(i, i ^ distance) for i in range(blocks)])
            distance *= 2
    else:
        scores = lax.psum(scores, "vocab")
    margin = (scores - teacher_margin) / (triples * groups)
    margin_all = in_group_order(other_groups(margin)).reshape(groups * triples)
    grads_all = by_term(in_group_order(other_groups(unscaled)).astype(jnp.float32))
    unscaled = unscaled.astype(jnp.float32)
    features_all = other_groups(features)

    head_terms = divisor(terms, 400)
    ranges = terms // head_terms
    next_range = 0
    grad_head = token = None

    def run_head(count, *waits):
        nonlocal grad_head, token, next_range
        if count == 0:
            return
        previous = [] if grad_head is None else [grad_head]
        start = next_range
        term_spec = pl.BlockSpec((head_terms, groups * docs), lambda r, d: (start + r, 0))
        grad_head, token = run(
            functools.partial(head_kernel, groups, docs),
            "head_terms",
            [margin_all, *features_all, places_all, grads_all, *previous],
            [index_spec]
            + [pl.BlockSpec((chunks, tokens, width), lambda r, d: (0, 0, d))] * groups
            + [term_spec] * 2
            + [any_spec] * len(previous),
            [jax.ShapeDtypeStruct((terms, depth), jnp.float32), jax.ShapeDtypeStruct((8, LANES), jnp.float32)],
            out_specs=[
                pl.BlockSpec((head_terms, block_width), lambda r, d: (start + r, d)),
                pl.BlockSpec((8, LANES), lambda r, d: (0, 0)),
            ],
            waits=waits,
            flops=count * 2 * groups * tokens * head_terms * depth // 4,
            aliases={3 + groups: 0} if previous else {},
            scratch=[pltpu.VMEM((head_terms, groups * tokens), jnp.bfloat16)],
            grid=(count, strips),
        )
        next_range += count

    parts = []
    for c in range(chunks):
        sums = run(
            functools.partial(hidden_kernel, docs, inner, strips, piece_shape),
            "hidden_terms",
            [head_rows] * strips + [places, unscaled],
            strip_specs(c) + [row_spec, row_spec],
            [bf16(*piece_shape)] * inner,
            out_specs=[piece_spec] * inner,
            waits=[parts[c - 3][-1] if c > 2 else None],
            flops=2 * tokens * strips * width * terms // 4,
            scratch=[
                pltpu.VMEM((tokens, columns), jnp.bfloat16),
                pltpu.VMEM((tokens, strips * width), jnp.float32),
            ],
            grid=(steps,),
        )
        parts.append([sums[0]] + [across_y(sums[q], q) for q in range(1, inner)])

    half = -(-chunks // 2)
    pairs = [pair for pair in (parts[:half], parts[half:]) if pair]
    share = ranges // 10
    mine_all = []
    arrived_all = []

    def add_blocks(pair, *waits):
        mine = run(
            functools.partial(combine_kernel, len(pair), inner, slots),
            "add_blocks",
            [value for each in pair for value in each],
            [vmem_spec] * (len(pair) * inner),
            [bf16(len(pair), near, docs, part, width)] * slots,
            waits=waits,
        )
        mine_all.append([mine[0]] + [lax.ppermute(mine[s], "seq", shift_perm(slots, s)) for s in range(1, slots)])

    def sort_pieces(mine, *waits):
        pieces = run(
            functools.partial(sort_kernel, slots, near, outer),
            "sort_pieces",
            mine,
            [vmem_spec] * slots,
            [bf16(mine[0].shape[0], docs, part, width)] * outer,
            waits=waits,
        )
        arrived_all.append([pieces[0]] + [across_z(pieces[ahead], ahead) for ahead in range(1, outer)])

    add_blocks(pairs[0])
    run_head(2 * share, mine_all[0][0], parts[-1][0])
    sort_pieces(mine_all[0], token)
    if len(pairs) > 1:
        add_blocks(pairs[1], arrived_all[0][0])
        run_head(2 * share, arrived_all[0][0], mine_all[1][0])
        sort_pieces(mine_all[1], token)
        run_head(share, arrived_all[1][0])
    run_head(ranges - next_range, *arrived_all[0][1:])
    (grad_hidden,) = run(
        functools.partial(finish_kernel, [len(pair) for pair in pairs], outer),
        "scale_hidden",
        [margin] + [value for arrived in arrived_all for value in arrived],
        [index_spec] + [vmem_spec] * (len(pairs) * outer),
        [bf16(docs, part, block_width)],
        waits=[token],
    )
    return (grad_head.T, grad_hidden)


def solution(mesh):
    axes = (mesh.shape["dp"], mesh.shape["seq"], mesh.shape["vocab"])
    return jax.shard_map(
        functools.partial(on_device, axes),
        mesh=mesh,
        in_specs=(
            P("dp", "seq", "vocab"),
            P("seq", "vocab"),
            P("dp", "vocab"),
            P("dp", "seq"),
            P("dp"),
        ),
        out_specs=(P("seq", "vocab"), P("dp", "seq", "vocab")),
        check_vma=False,
    )
```

```python
import functools

import jax
import jax.numpy as jnp
from jax import lax
from jax.experimental import pallas as pl
from jax.experimental.pallas import tpu as pltpu
from jax.sharding import PartitionSpec as P

LANES = 128
VMEM_BYTES = 48 * 1024 * 1024


def shift_perm(count, shift):
    return [(i, (i + shift) % count) for i in range(count)]


def waiting(kernel, count):
    return lambda *refs: kernel(refs[0], *refs[1 + count:])


def divisor(terms, limit):
    fits = [b for b in range(16, limit + 1, 16) if terms % b == 0]
    return fits[-1] if fits else terms


def ring_place(z, count):
    return jnp.where(lax.rem(z, 2) == 1, lax.div(z + 1, 2), jnp.where(z == 0, 0, count - lax.div(z, 2)))


def slice_kernel(index_ref, states_ref, out_ref):
    out_ref[...] = states_ref[...]


def pick_kernel(slots, near, outer, index_ref, *refs):
    held, outs = refs[:outer], refs[outer:]
    block_z, seq = index_ref[2], index_ref[3]
    for s in range(slots):
        half = lax.rem(seq + slots - s, slots)
        for n in range(near):
            back = lax.rem(ring_place(block_z, outer) + outer - ring_place(half * near + n, outer), outer)
            for b in range(outer):

                @pl.when(back == b)
                def _():
                    outs[s][n] = held[b][...]


def join_kernel(index_ref, *refs):
    for s in range(len(refs) - 1):
        refs[-1][s] = refs[s][...]


def logits_kernel(docs, inner, strips, *refs):
    index_ref = refs[0]
    pieces = refs[1:1 + inner]
    heads = refs[1 + inner:1 + inner + strips]
    places_ref = refs[1 + inner + strips]
    logits_ref, rows_ref = refs[-2:]
    slots, near, _, part, width = pieces[0].shape
    length = slots * part

    @pl.when(pl.program_id(0) == 0)
    def _():
        for q in range(inner):
            lane_y = lax.rem(index_ref[0] + q, inner)
            for n in range(near):
                lane = pl.multiple_of((n * inner + lane_y) * width, width)
                for k in range(docs):
                    for s in range(slots):
                        rows_ref[pl.ds(k * length + s * part, part), pl.ds(lane, width)] = pieces[q][s, n, k]

    head = jnp.concatenate([ref[...] for ref in heads], axis=1)
    dense = lax.dot_general(
        rows_ref[...], head, (((1,), (1,)), ((), ())), preferred_element_type=jnp.float32
    )
    token = lax.broadcasted_iota(jnp.int32, (length, head.shape[0]), 0)
    for k in range(docs):
        picked = jnp.where(token == places_ref[pl.ds(k, 1), :], dense[k * length:(k + 1) * length], 0.0)
        logits_ref[pl.ds(k, 1), :] = jnp.sum(picked, axis=0, keepdims=True)


def hidden_kernel(docs, inner, strips, shape, *refs):
    index_ref = refs[0]
    heads = refs[1:1 + strips]
    places_ref, grads_ref = refs[1 + strips:3 + strips]
    outs = refs[3 + strips:3 + strips + inner]
    spread_ref, total_ref = refs[-2:]
    count, slots, near, _, part, width = shape
    length = slots * part
    step = pl.program_id(0)
    head = jnp.concatenate([ref[...] for ref in heads], axis=1)
    token = lax.broadcasted_iota(jnp.int32, (length, head.shape[0]), 0)
    for k in range(docs):
        spread = jnp.where(token == places_ref[pl.ds(k, 1), :], grads_ref[pl.ds(k, 1), :], 0.0)
        spread_ref[pl.ds(k * length, length), :] = spread.astype(jnp.bfloat16)
    term = jnp.dot(spread_ref[...], head, preferred_element_type=jnp.float32)

    @pl.when(step == 0)
    def _():
        total_ref[...] = term

    @pl.when(step > 0)
    def _():
        total_ref[...] += term

    @pl.when(step == pl.num_programs(0) - 1)
    def _():
        for q in range(inner):
            lane_y = lax.rem(index_ref[0] + q, inner)
            for i in range(count):
                for n in range(near):
                    lane = pl.multiple_of(((i * near + n) * inner + lane_y) * width, width)
                    for k in range(docs):
                        for s in range(slots):
                            piece = total_ref[pl.ds(k * length + s * part, part), pl.ds(lane, width)]
                            outs[q][i, s, n, k] = piece.astype(jnp.bfloat16)


def combine_kernel(inner, slots, index_ref, *refs):
    parts, outs = refs[:inner], refs[inner:]
    for i in range(parts[0].shape[0]):
        for s in range(slots):
            total = parts[0][i, s].astype(jnp.float32)
            for other in parts[1:]:
                total = total + other[i, s].astype(jnp.float32)
            outs[s][i] = total.astype(jnp.bfloat16)


def columns_kernel(groups, index_ref, *refs):
    rows = refs[:groups]
    out_ref, turned_ref = refs[groups:]
    steps, docs, columns = rows[0].shape
    turned_ref[...] = jnp.zeros_like(turned_ref)
    for step in range(steps):
        for first in range(groups):

            @pl.when(index_ref[1] == first)
            def _():
                for g in range(groups):
                    place = (first + g) % groups * docs
                    turned_ref[place:place + docs, :columns] = rows[g][step]

        turned = turned_ref[...].T
        out_ref[step * columns:(step + 1) * columns, :] = turned[:columns, :groups * docs]


def sort_kernel(slots, near, outer, index_ref, *refs):
    mine, outs = refs[:slots], refs[slots:]
    block_z, seq = index_ref[2], index_ref[3]
    for ahead in range(outer):
        z = lax.rem(block_z + ahead, outer)
        slot = lax.rem(seq + slots - lax.div(z, near), slots)
        for s in range(slots):

            @pl.when(slot == s)
            def _():
                outs[ahead][...] = mine[s][:, lax.rem(z, near)]


def finish_kernel(counts, outer, index_ref, margin_ref, *refs):
    out_ref = refs[-1]
    docs = out_ref.shape[0]
    width = refs[0].shape[-1]
    c = 0
    for group, count in enumerate(counts):
        arrived = refs[group * outer:(group + 1) * outer]
        for i in range(count):
            for k in range(docs):
                total = arrived[0][i, k].astype(jnp.float32)
                for other in arrived[1:]:
                    total = total + other[i, k].astype(jnp.float32)
                out_ref[k, :, c * width:(c + 1) * width] = (total * margin_ref[k // 3]).astype(jnp.bfloat16)
            c += 1


def head_kernel(groups, docs, *refs):
    index_ref, margin_ref = refs[:2]
    rows = refs[2:2 + groups]
    places_ref, grads_ref = refs[2 + groups:4 + groups]
    out_ref, token_ref, spread_ref = refs[-3:]
    chunks, tokens, width = rows[0].shape
    length = tokens // docs

    @pl.when(pl.program_id(1) == 0)
    def _():
        token_ref[...] = jnp.zeros_like(token_ref)
        token = lax.broadcasted_iota(jnp.int32, (out_ref.shape[0], length), 1)
        for k in range(groups * docs):
            grads = grads_ref[:, k:k + 1] * margin_ref[k // 3]
            spread = jnp.where(token == places_ref[:, k:k + 1], grads, 0.0)
            spread_ref[:, k * length:(k + 1) * length] = spread.astype(jnp.bfloat16)

    for first in range(groups):

        @pl.when(index_ref[1] == first)
        def _():
            total = None
            for g in range(groups):
                ref = rows[(g - first) % groups]
                features = jnp.concatenate([ref[c] for c in range(chunks)], axis=1)
                term = jnp.dot(
                    spread_ref[:, g * tokens:(g + 1) * tokens], features, preferred_element_type=jnp.float32
                )
                total = term if total is None else total + term
            out_ref[...] = total


def on_device(axes, hidden_states, head_weight, owner_pos, token_ids, teacher_margin):
    groups, slots, blocks = axes
    docs, part, block_width = hidden_states.shape
    depth, terms = head_weight.shape
    triples = teacher_margin.shape[0]
    inner = 2 if blocks % 2 == 0 else 1
    outer = blocks // inner
    near = outer // slots
    chunks = max(1, block_width // LANES)
    width = block_width // chunks
    length = slots * part
    tokens = docs * length
    columns = divisor(terms, 2048)
    steps = terms // columns
    strips = near * inner

    group = lax.axis_index("dp")
    seq = lax.axis_index("seq")
    block = lax.axis_index("vocab")
    block_y = lax.rem(block, inner)
    block_z = lax.div(block, inner)
    index = jnp.stack([block_y, group, block_z, seq]).astype(jnp.int32)

    def across_y(value, shift):
        perm = [(z * inner + y, z * inner + (y + shift) % inner) for z in range(outer) for y in range(inner)]
        return lax.ppermute(value, "vocab", perm)

    order = [0] + list(range(1, outer, 2)) + [z for z in range(outer - 1, 0, -1) if z % 2 == 0]
    ring = [(order[p] * inner + y, order[(p + 1) % outer] * inner + y) for p in range(outer) for y in range(inner)]

    def across_z(value, shift):
        perm = [(z * inner + y, (z + shift) % outer * inner + y) for z in range(outer) for y in range(inner)]
        return lax.ppermute(value, "vocab", perm)

    def other_groups(value):
        return [value] + [lax.ppermute(value, "dp", shift_perm(groups, -g)) for g in range(1, groups)]

    def in_group_order(values):
        doubled = jnp.stack(values + values)
        return lax.dynamic_slice_in_dim(doubled, lax.rem(groups - group, groups), groups, axis=0)

    def by_term(value):
        return value.transpose(1, 3, 0, 2).reshape(terms, groups * docs)

    def blocked(value):
        return value.reshape(docs, steps, columns).transpose(1, 0, 2)

    head_rows = head_weight.T
    strip_specs = lambda c: [
        pl.BlockSpec((columns, width), functools.partial(lambda lane, v: (v, lane), strip * chunks + c))
        for strip in range(strips)
    ]
    row_spec = pl.BlockSpec((pl.squeezed, docs, columns), lambda v: (v, 0, 0))
    piece_shape = (slots, near, docs, part, width)
    piece_spec = pl.BlockSpec(piece_shape, lambda v: (0, 0, 0, 0, 0))
    index_spec = pl.BlockSpec(memory_space=pltpu.SMEM)
    vmem_spec = pl.BlockSpec(memory_space=pltpu.VMEM)
    any_spec = pl.BlockSpec(memory_space=pl.ANY)
    params = pltpu.CompilerParams(vmem_limit_bytes=VMEM_BYTES)

    def cost(flops, transferred):
        return pl.CostEstimate(flops=int(flops), bytes_accessed=int(transferred), transcendentals=0)

    owner_blocks = blocked(owner_pos)
    places = lax.rem(owner_blocks + (length - seq * part), length)
    own_lengths = jnp.sum((token_ids != 0).astype(jnp.int32), axis=1, keepdims=True)
    lengths = own_lengths
    for s in range(1, slots):
        lengths = lengths + lax.ppermute(own_lengths, "seq", shift_perm(slots, s))
    validity = (owner_blocks < lengths[None]).astype(jnp.float32)
    places_all = by_term(in_group_order(other_groups(places)))

    def run(kernel, name, operands, specs, shapes, out_specs=None, waits=(), flops=0, aliases={}, scratch=(), grid=()):
        waits = [value for value in waits if value is not None]
        return pl.pallas_call(
            waiting(kernel, len(waits)),
            grid=grid,
            in_specs=[index_spec] + [any_spec] * len(waits) + specs,
            out_specs=out_specs or [vmem_spec] * len(shapes),
            out_shape=shapes,
            scratch_shapes=list(scratch),
            input_output_aliases={1 + len(waits) + i: o for i, o in aliases.items()},
            compiler_params=params,
            cost_estimate=cost(flops, flops // 64),
            name=name,
        )(index, *waits, *operands)

    bf16 = lambda *shape: jax.ShapeDtypeStruct(shape, jnp.bfloat16)
    moved_shape = bf16(near, docs, part, width)
    gathered_chunks = []
    others = []
    first_step = None
    for c in range(chunks):
        (own,) = run(
            slice_kernel,
            "feature_chunk",
            [hidden_states],
            [pl.BlockSpec((docs, part, width), functools.partial(lambda c, i: (0, 0, c), c))],
            [bf16(docs, part, width)],
            out_specs=[pl.BlockSpec((docs, part, width), lambda i: (0, 0, 0))],
            waits=[first_step],
            grid=(1,),
        )
        held = [own]
        for _ in range(outer - 1):
            held.append(lax.ppermute(held[-1], "vocab", ring))
        first_step = held[min(1, outer - 1)]
        mine, *sends = run(
            functools.partial(pick_kernel, slots, near, outer),
            "pick_halves",
            held,
            [vmem_spec] * outer,
            [moved_shape] * slots,
            waits=[gathered_chunks[c - 2] if c > 1 else None],
        )
        arrived = [lax.ppermute(sends[s - 1], "seq", shift_perm(slots, -s)) for s in range(1, slots)]
        (gathered,) = run(
            join_kernel,
            "join_tokens",
            [mine, *arrived],
            [vmem_spec] * slots,
            [bf16(*piece_shape)],
            waits=[others[c - 2] if c > 1 else None],
        )
        gathered_chunks.append(gathered)
        others.append(across_y(gathered, -1) if inner > 1 else None)

    logit_parts = []
    features = None
    for c in range(chunks):
        pieces = [gathered_chunks[c], others[c]][:inner]
        previous = [] if features is None else [features]
        chunk_logits, features = run(
            functools.partial(logits_kernel, docs, inner, strips),
            "pooled_logits",
            [*pieces, *[head_rows] * strips, places, *previous],
            [piece_spec] * inner + strip_specs(c) + [row_spec] + [any_spec] * len(previous),
            [
                jax.ShapeDtypeStruct((steps, docs, columns), jnp.float32),
                bf16(chunks, tokens, strips * width),
            ],
            out_specs=[
                row_spec,
                pl.BlockSpec(
                    (pl.squeezed, tokens, strips * width), functools.partial(lambda c, v: (c, 0, 0), c)
                ),
            ],
            waits=[places_all, gathered_chunks[-1]] if c == 0 else [validity, others[-2]] if c == 1 else [],
            flops=2 * tokens * strips * width * terms,
            aliases={inner + strips + 1: 1} if previous else {},
            grid=(steps,),
        )
        logit_parts.append(chunk_logits)

    logit_part = functools.reduce(jnp.add, logit_parts)
    logits = logit_part
    for s in range(1, slots):
        logits = logits + lax.ppermute(logit_part, "seq", shift_perm(slots, s))
    softened = jax.nn.softplus(logits)
    pooled = validity * jnp.log1p(softened)
    slopes = validity * jax.nn.sigmoid(logits) / (1.0 + softened)
    view = pooled.reshape(steps, triples, 3, columns)
    query, positive, negative = view[:, :, 0], view[:, :, 1], view[:, :, 2]
    unscaled = jnp.stack([positive - negative, query, -query], axis=2).reshape(logits.shape) * slopes
    unscaled = unscaled.astype(jnp.bfloat16)
    unscaled = unscaled.astype(jnp.float32)
    scores = jnp.sum(query * positive, axis=(0, 2)) - jnp.sum(query * negative, axis=(0, 2))
    score_row = jnp.pad(scores, (0, columns - triples)).reshape(1, 1, columns)
    packed = jnp.concatenate([unscaled, jnp.broadcast_to(score_row, (steps, 1, columns))], axis=1)
    packed_all = other_groups(packed)
    scores = in_group_order([scores] + [value[0, docs, :triples] for value in packed_all[1:]])
    if blocks & (blocks - 1) == 0:
        distance = 1
        while distance < blocks:
            scores = scores + lax.ppermute(scores, "vocab", [(i, i ^ distance) for i in range(blocks)])
            distance *= 2
    else:
        scores = lax.psum(scores, "vocab")
    margin_all = ((scores - in_group_order(other_groups(teacher_margin))) / (triples * groups)).reshape(-1)
    margin = lax.dynamic_slice(margin_all, (group * triples,), (triples,))
    (grads_all,) = run(
        functools.partial(columns_kernel, groups),
        "turn_gradients",
        [unscaled] + [value[:, :docs] for value in packed_all[1:]],
        [vmem_spec] * groups,
        [jax.ShapeDtypeStruct((terms, groups * docs), jnp.float32)],
        scratch=[pltpu.VMEM((-(-groups * docs // 8) * 8, -(-columns // LANES) * LANES), jnp.float32)],
    )
    features_all = other_groups(features)

    head_terms = divisor(terms, 800)
    ranges = terms // head_terms
    next_range = 0
    grad_head = token = None

    def run_head(count, *waits):
        nonlocal grad_head, token, next_range
        if count == 0:
            return
        previous = [] if grad_head is None else [grad_head]
        start = next_range
        term_spec = pl.BlockSpec((head_terms, groups * docs), lambda r, d: (start + r, 0))
        grad_head, token = run(
            functools.partial(head_kernel, groups, docs),
            "head_terms",
            [margin_all, *features_all, places_all, grads_all, *previous],
            [index_spec]
            + [pl.BlockSpec((chunks, tokens, width), lambda r, d: (0, 0, d))] * groups
            + [term_spec] * 2
            + [any_spec] * len(previous),
            [jax.ShapeDtypeStruct((terms, depth), jnp.float32), jax.ShapeDtypeStruct((8, LANES), jnp.float32)],
            out_specs=[
                pl.BlockSpec((head_terms, block_width), lambda r, d: (start + r, d)),
                pl.BlockSpec((8, LANES), lambda r, d: (0, 0)),
            ],
            waits=waits,
            flops=count * 2 * groups * tokens * head_terms * depth // 4,
            aliases={3 + groups: 0} if previous else {},
            scratch=[pltpu.VMEM((head_terms, groups * tokens), jnp.bfloat16)],
            grid=(count, strips),
        )
        next_range += count

    half = -(-chunks // 2)
    chunk_groups = [members for members in (range(half), range(half, chunks)) if members]
    pairs = []
    for members in chunk_groups:
        pair_shape = (len(members), *piece_shape)
        lanes = len(members) * strips * width
        sums = run(
            functools.partial(hidden_kernel, docs, inner, len(members) * strips, pair_shape),
            "hidden_terms",
            [head_rows] * (len(members) * strips) + [places, unscaled],
            [spec for c in members for spec in strip_specs(c)] + [row_spec, row_spec],
            [bf16(*pair_shape)] * inner,
            out_specs=[pl.BlockSpec(pair_shape, lambda v: (0,) * 6)] * inner,
            flops=2 * tokens * lanes * terms // 4,
            scratch=[pltpu.VMEM((tokens, columns), jnp.bfloat16), pltpu.VMEM((tokens, lanes), jnp.float32)],
            grid=(steps,),
        )
        pairs.append([sums[0]] + [across_y(sums[q], q) for q in range(1, inner)])

    share = ranges // 5
    mine_all = []
    arrived_all = []

    def add_blocks(pair, *waits):
        count = pair[0].shape[0]
        mine = run(
            functools.partial(combine_kernel, inner, slots),
            "add_blocks",
            pair,
            [vmem_spec] * inner,
            [bf16(count, near, docs, part, width)] * slots,
            waits=waits,
        )
        mine_all.append([mine[0]] + [lax.ppermute(mine[s], "seq", shift_perm(slots, s)) for s in range(1, slots)])

    def sort_pieces(mine, *waits):
        pieces = run(
            functools.partial(sort_kernel, slots, near, outer),
            "sort_pieces",
            mine,
            [vmem_spec] * slots,
            [bf16(mine[0].shape[0], docs, part, width)] * outer,
            waits=waits,
        )
        arrived_all.append([pieces[0]] + [across_z(pieces[ahead], ahead) for ahead in range(1, outer)])

    add_blocks(pairs[0])
    run_head(2 * share, mine_all[0][0], pairs[-1][0])
    sort_pieces(mine_all[0], token)
    if len(pairs) > 1:
        add_blocks(pairs[1], arrived_all[0][0])
        run_head(share, arrived_all[0][0], mine_all[1][0])
        sort_pieces(mine_all[1], token)
    run_head(ranges - next_range, arrived_all[-1][0])
    (grad_hidden,) = run(
        functools.partial(finish_kernel, [len(members) for members in chunk_groups], outer),
        "scale_hidden",
        [margin] + [value for arrived in arrived_all for value in arrived],
        [index_spec] + [vmem_spec] * (len(pairs) * outer),
        [bf16(docs, part, block_width)],
        waits=[token],
    )
    return (grad_head.T, grad_hidden)


def solution(mesh):
    axes = (mesh.shape["dp"], mesh.shape["seq"], mesh.shape["vocab"])
    return jax.shard_map(
        functools.partial(on_device, axes),
        mesh=mesh,
        in_specs=(
            P("dp", "seq", "vocab"),
            P("seq", "vocab"),
            P("dp", "vocab"),
            P("dp", "seq"),
            P("dp"),
        ),
        out_specs=(P("seq", "vocab"), P("dp", "seq", "vocab")),
        check_vma=False,
    )
```

```python
import functools

import jax
import jax.numpy as jnp
from jax import lax
from jax.experimental import pallas as pl
from jax.experimental.pallas import tpu as pltpu
from jax.sharding import PartitionSpec as P

LANES = 128
VMEM_BYTES = 48 * 1024 * 1024


def shift_perm(count, shift):
    return [(i, (i + shift) % count) for i in range(count)]


def waiting(kernel, count):
    return lambda *refs: kernel(refs[0], *refs[1 + count:])


def divisor(terms, limit):
    fits = [b for b in range(16, limit + 1, 16) if terms % b == 0]
    return fits[-1] if fits else terms


def ring_place(z, count):
    return jnp.where(lax.rem(z, 2) == 1, lax.div(z + 1, 2), jnp.where(z == 0, 0, count - lax.div(z, 2)))


def copy_kernel(index_ref, states_ref, out_ref):
    out_ref[...] = states_ref[...]


def pick_kernel(slots, near, outer, index_ref, *refs):
    held, outs = refs[:outer], refs[outer:]
    block_z, seq = index_ref[2], index_ref[3]
    for s in range(slots):
        half = lax.rem(seq + slots - s, slots)
        for n in range(near):
            back = lax.rem(ring_place(block_z, outer) + outer - ring_place(half * near + n, outer), outer)
            for b in range(outer):

                @pl.when(back == b)
                def _():
                    outs[s][n] = held[b][...]


def join_kernel(index_ref, *refs):
    for s in range(len(refs) - 1):
        refs[-1][s] = refs[s][...]


def logits_kernel(docs, inner, strips, *refs):
    index_ref = refs[0]
    pieces = refs[1:1 + inner]
    heads = refs[1 + inner:1 + inner + strips]
    places_ref = refs[1 + inner + strips]
    logits_ref, rows_ref = refs[-2:]
    slots, near, _, part, width = pieces[0].shape
    length = slots * part

    @pl.when(pl.program_id(0) == 0)
    def _():
        for q in range(inner):
            lane_y = lax.rem(index_ref[0] + q, inner)
            for n in range(near):
                lane = pl.multiple_of((n * inner + lane_y) * width, width)
                for k in range(docs):
                    for s in range(slots):
                        rows_ref[pl.ds(k * length + s * part, part), pl.ds(lane, width)] = pieces[q][s, n, k]

    head = jnp.concatenate([ref[...] for ref in heads], axis=1)
    dense = lax.dot_general(
        rows_ref[...], head, (((1,), (1,)), ((), ())), preferred_element_type=jnp.float32
    )
    token = lax.broadcasted_iota(jnp.int32, (length, head.shape[0]), 0)
    for k in range(docs):
        picked = jnp.where(token == places_ref[pl.ds(k, 1), :], dense[k * length:(k + 1) * length], 0.0)
        logits_ref[pl.ds(k, 1), :] = jnp.sum(picked, axis=0, keepdims=True)


def hidden_kernel(docs, inner, strips, shape, *refs):
    index_ref = refs[0]
    heads = refs[1:1 + strips]
    places_ref, grads_ref = refs[1 + strips:3 + strips]
    outs = refs[3 + strips:3 + strips + inner]
    spread_ref, total_ref = refs[-2:]
    count, slots, near, _, part, width = shape
    length = slots * part
    step = pl.program_id(0)
    head = jnp.concatenate([ref[...] for ref in heads], axis=1)
    token = lax.broadcasted_iota(jnp.int32, (length, head.shape[0]), 0)
    for k in range(docs):
        spread = jnp.where(token == places_ref[pl.ds(k, 1), :], grads_ref[pl.ds(k, 1), :], 0.0)
        spread_ref[pl.ds(k * length, length), :] = spread.astype(jnp.bfloat16)
    term = jnp.dot(spread_ref[...], head, preferred_element_type=jnp.float32)

    @pl.when(step == 0)
    def _():
        total_ref[...] = term

    @pl.when(step > 0)
    def _():
        total_ref[...] += term

    @pl.when(step == pl.num_programs(0) - 1)
    def _():
        for q in range(inner):
            lane_y = lax.rem(index_ref[0] + q, inner)
            for i in range(count):
                for n in range(near):
                    lane = pl.multiple_of(((i * near + n) * inner + lane_y) * width, width)
                    for k in range(docs):
                        for s in range(slots):
                            piece = total_ref[pl.ds(k * length + s * part, part), pl.ds(lane, width)]
                            outs[q][i, s, n, k] = piece.astype(jnp.bfloat16)


def combine_kernel(inner, slots, index_ref, *refs):
    parts, outs = refs[:inner], refs[inner:]
    for i in range(parts[0].shape[0]):
        for s in range(slots):
            total = parts[0][i, s].astype(jnp.float32)
            for other in parts[1:]:
                total = total + other[i, s].astype(jnp.float32)
            outs[s][i] = total.astype(jnp.bfloat16)


def columns_kernel(groups, docs, index_ref, *refs):
    packed = refs[:groups]
    out_ref, turned_ref = refs[groups:]
    steps, _, columns = packed[0].shape
    count = groups * docs
    turned_ref[...] = jnp.zeros_like(turned_ref)
    for step in range(steps):
        for first in range(groups):

            @pl.when(index_ref[1] == first)
            def _():
                for g in range(groups):
                    place = (first + g) % groups * docs
                    turned_ref[place:place + docs, :columns] = packed[g][step, :docs]
                    turned_ref[count + place:count + place + docs, :columns] = packed[g][step, docs:2 * docs]

        turned = turned_ref[...].T
        out_ref[step * columns:(step + 1) * columns, :] = turned[:columns, :2 * count]


def sort_kernel(slots, near, outer, index_ref, *refs):
    mine, outs = refs[:slots], refs[slots:]
    block_z, seq = index_ref[2], index_ref[3]
    for ahead in range(outer):
        z = lax.rem(block_z + ahead, outer)
        slot = lax.rem(seq + slots - lax.div(z, near), slots)
        for s in range(slots):

            @pl.when(slot == s)
            def _():
                outs[ahead][...] = mine[s][:, lax.rem(z, near)]


def finish_kernel(counts, outer, index_ref, margin_ref, *refs):
    out_ref = refs[-1]
    docs = out_ref.shape[0]
    width = refs[0].shape[-1]
    c = 0
    for group, count in enumerate(counts):
        arrived = refs[group * outer:(group + 1) * outer]
        for i in range(count):
            for k in range(docs):
                total = arrived[0][i, k].astype(jnp.float32)
                for other in arrived[1:]:
                    total = total + other[i, k].astype(jnp.float32)
                out_ref[k, :, c * width:(c + 1) * width] = (total * margin_ref[k // 3]).astype(jnp.bfloat16)
            c += 1


def head_kernel(groups, docs, *refs):
    index_ref, margin_ref = refs[:2]
    rows = refs[2:2 + groups]
    columns_ref = refs[2 + groups]
    out_ref, token_ref, spread_ref = refs[-3:]
    chunks, tokens, width = rows[0].shape
    length = tokens // docs
    count = groups * docs

    @pl.when(pl.program_id(1) == 0)
    def _():
        token_ref[...] = jnp.zeros_like(token_ref)
        token = lax.broadcasted_iota(jnp.int32, (out_ref.shape[0], length), 1).astype(jnp.float32)
        for k in range(count):
            grads = columns_ref[:, k:k + 1] * margin_ref[k // 3]
            spread = jnp.where(token == columns_ref[:, count + k:count + k + 1], grads, 0.0)
            spread_ref[:, k * length:(k + 1) * length] = spread.astype(jnp.bfloat16)

    for first in range(groups):

        @pl.when(index_ref[1] == first)
        def _():
            total = None
            for g in range(groups):
                ref = rows[(g - first) % groups]
                features = jnp.concatenate([ref[c] for c in range(chunks)], axis=1)
                term = jnp.dot(
                    spread_ref[:, g * tokens:(g + 1) * tokens], features, preferred_element_type=jnp.float32
                )
                total = term if total is None else total + term
            out_ref[...] = total


def on_device(axes, hidden_states, head_weight, owner_pos, token_ids, teacher_margin):
    groups, slots, blocks = axes
    docs, part, block_width = hidden_states.shape
    depth, terms = head_weight.shape
    triples = teacher_margin.shape[0]
    inner = 2 if blocks % 2 == 0 else 1
    outer = blocks // inner
    near = outer // slots
    chunks = max(1, block_width // LANES)
    width = block_width // chunks
    length = slots * part
    tokens = docs * length
    columns = divisor(terms, 2048)
    steps = terms // columns
    strips = near * inner

    group = lax.axis_index("dp")
    seq = lax.axis_index("seq")
    block = lax.axis_index("vocab")
    block_y = lax.rem(block, inner)
    block_z = lax.div(block, inner)
    index = jnp.stack([block_y, group, block_z, seq]).astype(jnp.int32)

    def across_y(value, shift):
        perm = [(z * inner + y, z * inner + (y + shift) % inner) for z in range(outer) for y in range(inner)]
        return lax.ppermute(value, "vocab", perm)

    order = [0] + list(range(1, outer, 2)) + [z for z in range(outer - 1, 0, -1) if z % 2 == 0]

    def around_ring(value, steps_on):
        perm = [
            (order[p] * inner + y, order[(p + steps_on) % outer] * inner + y)
            for p in range(outer)
            for y in range(inner)
        ]
        return lax.ppermute(value, "vocab", perm)

    def across_z(value, shift):
        perm = [(z * inner + y, (z + shift) % outer * inner + y) for z in range(outer) for y in range(inner)]
        return lax.ppermute(value, "vocab", perm)

    def other_groups(value):
        return [value] + [lax.ppermute(value, "dp", shift_perm(groups, -g)) for g in range(1, groups)]

    def in_group_order(values):
        doubled = jnp.stack(values + values)
        return lax.dynamic_slice_in_dim(doubled, lax.rem(groups - group, groups), groups, axis=0)

    def blocked(value):
        return value.reshape(docs, steps, columns).transpose(1, 0, 2)

    head_rows = head_weight.T
    strip_specs = lambda c: [
        pl.BlockSpec((columns, width), functools.partial(lambda lane, v: (v, lane), strip * chunks + c))
        for strip in range(strips)
    ]
    row_spec = pl.BlockSpec((pl.squeezed, docs, columns), lambda v: (v, 0, 0))
    piece_shape = (slots, near, docs, part, width)
    piece_spec = pl.BlockSpec(piece_shape, lambda v: (0, 0, 0, 0, 0))
    index_spec = pl.BlockSpec(memory_space=pltpu.SMEM)
    vmem_spec = pl.BlockSpec(memory_space=pltpu.VMEM)
    any_spec = pl.BlockSpec(memory_space=pl.ANY)
    params = pltpu.CompilerParams(vmem_limit_bytes=VMEM_BYTES)

    def cost(flops, transferred):
        return pl.CostEstimate(flops=int(flops), bytes_accessed=int(transferred), transcendentals=0)

    owner_blocks = blocked(owner_pos)
    places = lax.rem(owner_blocks + (length - seq * part), length)
    own_lengths = jnp.sum((token_ids != 0).astype(jnp.int32), axis=1, keepdims=True)
    lengths = own_lengths
    for s in range(1, slots):
        lengths = lengths + lax.ppermute(own_lengths, "seq", shift_perm(slots, s))
    validity = (owner_blocks < lengths[None]).astype(jnp.float32)

    def run(kernel, name, operands, specs, shapes, out_specs=None, waits=(), flops=0, aliases={}, scratch=(), grid=()):
        waits = [value for value in waits if value is not None]
        return pl.pallas_call(
            waiting(kernel, len(waits)),
            grid=grid,
            in_specs=[index_spec] + [any_spec] * len(waits) + specs,
            out_specs=out_specs or [vmem_spec] * len(shapes),
            out_shape=shapes,
            scratch_shapes=list(scratch),
            input_output_aliases={1 + len(waits) + i: o for i, o in aliases.items()},
            compiler_params=params,
            cost_estimate=cost(flops, flops // 64),
            name=name,
        )(index, *waits, *operands)

    bf16 = lambda *shape: jax.ShapeDtypeStruct(shape, jnp.bfloat16)
    moved_shape = bf16(near, docs, part, width)
    sliced = [hidden_states[:, :, c * width:(c + 1) * width] for c in range(chunks)]
    last = chunks - 1
    gathered_chunks = []
    others = []
    logit_parts = []
    features = None

    def add_logits(c, waits):
        nonlocal features
        previous = [] if features is None else [features]
        chunk_logits, features = run(
            functools.partial(logits_kernel, docs, inner, strips),
            "pooled_logits",
            [gathered_chunks[c], others[c]][:inner] + [head_rows] * strips + [places, *previous],
            [piece_spec] * inner + strip_specs(c) + [row_spec] + [any_spec] * len(previous),
            [
                jax.ShapeDtypeStruct((steps, docs, columns), jnp.float32),
                bf16(chunks, tokens, strips * width),
            ],
            out_specs=[
                row_spec,
                pl.BlockSpec(
                    (pl.squeezed, tokens, strips * width), functools.partial(lambda c, v: (c, 0, 0), c)
                ),
            ],
            waits=waits,
            flops=2 * tokens * strips * width * terms,
            aliases={inner + strips + 1: 1} if previous else {},
            grid=(steps,),
        )
        logit_parts.append(chunk_logits)

    first_step = None
    for c in range(chunks):
        own = sliced[c]
        if c > 0:
            (own,) = run(
                copy_kernel, "feature_chunk", [own], [vmem_spec], [bf16(docs, part, width)], waits=[first_step]
            )
        held = [own]
        for back in range(1, outer):
            held.append(around_ring(own, back) if c == 0 else around_ring(held[-1], 1))
        first_step = held[min(1, outer - 1)]
        mine, *sends = run(
            functools.partial(pick_kernel, slots, near, outer),
            "pick_halves",
            held,
            [vmem_spec] * outer,
            [moved_shape] * slots,
            waits=[gathered_chunks[c - 1] if c > 0 else None],
        )
        arrived = [lax.ppermute(sends[s - 1], "seq", shift_perm(slots, -s)) for s in range(1, slots)]
        if c == last and c > 1:
            add_logits(0, [mine])
        (gathered,) = run(
            join_kernel,
            "join_tokens",
            [mine, *arrived],
            [vmem_spec] * slots,
            [bf16(*piece_shape)],
            waits=[others[c - 2] if c > 1 else None, logit_parts[0] if logit_parts else None],
        )
        gathered_chunks.append(gathered)
        others.append(across_y(gathered, -1) if inner > 1 else None)
    for c in range(len(logit_parts), chunks):
        add_logits(c, [validity, others[-2]] if c == 1 else [])

    logit_part = functools.reduce(jnp.add, logit_parts)
    logits = logit_part
    for s in range(1, slots):
        logits = logits + lax.ppermute(logit_part, "seq", shift_perm(slots, s))
    softened = jax.nn.softplus(logits)
    pooled = validity * jnp.log1p(softened)
    slopes = validity * jax.nn.sigmoid(logits) / (1.0 + softened)
    view = pooled.reshape(steps, triples, 3, columns)
    query, positive, negative = view[:, :, 0], view[:, :, 1], view[:, :, 2]
    unscaled = jnp.stack([positive - negative, query, -query], axis=2).reshape(logits.shape) * slopes
    unscaled = unscaled.astype(jnp.bfloat16)
    unscaled = unscaled.astype(jnp.float32)
    scores = jnp.sum(query * positive, axis=(0, 2)) - jnp.sum(query * negative, axis=(0, 2))
    paired = blocks & (blocks - 1) == 0
    distance = 1

    def add_distance(value, distance):
        return value + lax.ppermute(value, "vocab", [(i, i ^ distance) for i in range(blocks)])

    if paired and blocks > 1:
        scores = add_distance(scores, distance)
        distance *= 2
    score_row = jnp.pad(jnp.concatenate([scores, teacher_margin]), (0, columns - 2 * triples))
    packed = jnp.concatenate(
        [unscaled, places.astype(jnp.float32), jnp.broadcast_to(score_row, (steps, 1, columns))], axis=1
    )
    packed_all = other_groups(packed)
    scores = in_group_order([scores] + [value[0, 2 * docs, :triples] for value in packed_all[1:]])
    teacher = in_group_order([teacher_margin] + [value[0, 2 * docs, triples:2 * triples] for value in packed_all[1:]])
    if paired:
        while distance < blocks:
            scores = add_distance(scores, distance)
            distance *= 2
    else:
        scores = lax.psum(scores, "vocab")
    margin_all = ((scores - teacher) / (triples * groups)).reshape(-1)
    margin = lax.dynamic_slice(margin_all, (group * triples,), (triples,))
    (head_columns,) = run(
        functools.partial(columns_kernel, groups, docs),
        "turn_gradients",
        packed_all,
        [vmem_spec] * groups,
        [jax.ShapeDtypeStruct((terms, 2 * groups * docs), jnp.float32)],
        scratch=[pltpu.VMEM((-(-2 * groups * docs // 8) * 8, -(-columns // LANES) * LANES), jnp.float32)],
    )
    features_all = other_groups(features)

    head_terms = divisor(terms, 800)
    ranges = terms // head_terms
    next_range = 0
    grad_head = token = None

    def run_head(count, *waits):
        nonlocal grad_head, token, next_range
        if count == 0:
            return
        previous = [] if grad_head is None else [grad_head]
        start = next_range
        term_spec = pl.BlockSpec((head_terms, 2 * groups * docs), lambda r, d: (start + r, 0))
        grad_head, token = run(
            functools.partial(head_kernel, groups, docs),
            "head_terms",
            [margin_all, *features_all, head_columns, *previous],
            [index_spec]
            + [pl.BlockSpec((chunks, tokens, width), lambda r, d: (0, 0, d))] * groups
            + [term_spec]
            + [any_spec] * len(previous),
            [jax.ShapeDtypeStruct((terms, depth), jnp.float32), jax.ShapeDtypeStruct((8, LANES), jnp.float32)],
            out_specs=[
                pl.BlockSpec((head_terms, block_width), lambda r, d: (start + r, d)),
                pl.BlockSpec((8, LANES), lambda r, d: (0, 0)),
            ],
            waits=waits,
            flops=count * 2 * groups * tokens * head_terms * depth // 4,
            aliases={2 + groups: 0} if previous else {},
            scratch=[pltpu.VMEM((head_terms, groups * tokens), jnp.bfloat16)],
            grid=(count, strips),
        )
        next_range += count

    half = -(-chunks // 2)
    chunk_groups = [members for members in (range(half), range(half, chunks)) if members]
    pairs = []
    for members in chunk_groups:
        pair_shape = (len(members), *piece_shape)
        lanes = len(members) * strips * width
        sums = run(
            functools.partial(hidden_kernel, docs, inner, len(members) * strips, pair_shape),
            "hidden_terms",
            [head_rows] * (len(members) * strips) + [places, unscaled],
            [spec for c in members for spec in strip_specs(c)] + [row_spec, row_spec],
            [bf16(*pair_shape)] * inner,
            out_specs=[pl.BlockSpec(pair_shape, lambda v: (0,) * 6)] * inner,
            waits=[packed] if pairs else [],
            flops=2 * tokens * lanes * terms // 4,
            scratch=[pltpu.VMEM((tokens, columns), jnp.bfloat16), pltpu.VMEM((tokens, lanes), jnp.float32)],
            grid=(steps,),
        )
        pairs.append([sums[0]] + [across_y(sums[q], q) for q in range(1, inner)])

    share = ranges // 5
    mine_all = []
    arrived_all = []

    def add_blocks(pair, *waits):
        count = pair[0].shape[0]
        mine = run(
            functools.partial(combine_kernel, inner, slots),
            "add_blocks",
            pair,
            [vmem_spec] * inner,
            [bf16(count, near, docs, part, width)] * slots,
            waits=waits,
        )
        mine_all.append([mine[0]] + [lax.ppermute(mine[s], "seq", shift_perm(slots, s)) for s in range(1, slots)])

    def sort_pieces(mine, *waits):
        pieces = run(
            functools.partial(sort_kernel, slots, near, outer),
            "sort_pieces",
            mine,
            [vmem_spec] * slots,
            [bf16(mine[0].shape[0], docs, part, width)] * outer,
            waits=waits,
        )
        arrived_all.append([pieces[0]] + [across_z(pieces[ahead], ahead) for ahead in range(1, outer)])

    add_blocks(pairs[0])
    run_head(2 * share, mine_all[0][0], pairs[-1][0])
    sort_pieces(mine_all[0], token)
    if len(pairs) > 1:
        add_blocks(pairs[1], arrived_all[0][0])
        run_head(share, arrived_all[0][0], mine_all[1][0])
        sort_pieces(mine_all[1], token)
    run_head(ranges - next_range, arrived_all[-1][0])
    (grad_hidden,) = run(
        functools.partial(finish_kernel, [len(members) for members in chunk_groups], outer),
        "scale_hidden",
        [margin] + [value for arrived in arrived_all for value in arrived],
        [index_spec] + [vmem_spec] * (len(pairs) * outer),
        [bf16(docs, part, block_width)],
        waits=[token],
    )
    return (grad_head.T, grad_hidden)


def solution(mesh):
    axes = (mesh.shape["dp"], mesh.shape["seq"], mesh.shape["vocab"])
    return jax.shard_map(
        functools.partial(on_device, axes),
        mesh=mesh,
        in_specs=(
            P("dp", "seq", "vocab"),
            P("seq", "vocab"),
            P("dp", "vocab"),
            P("dp", "seq"),
            P("dp"),
        ),
        out_specs=(P("seq", "vocab"), P("dp", "seq", "vocab")),
        check_vma=False,
    )
```

```python
import functools

import jax
import jax.numpy as jnp
from jax import lax
from jax.experimental import pallas as pl
from jax.experimental.pallas import tpu as pltpu
from jax.sharding import PartitionSpec as P

LANES = 128
VMEM_BYTES = 48 * 1024 * 1024


def shift_perm(count, shift):
    return [(i, (i + shift) % count) for i in range(count)]


def waiting(kernel, count):
    return lambda *refs: kernel(refs[0], *refs[1 + count:])


def divisor(terms, limit):
    fits = [b for b in range(16, limit + 1, 16) if terms % b == 0]
    return fits[-1] if fits else terms


def ring_place(z, count):
    return jnp.where(lax.rem(z, 2) == 1, lax.div(z + 1, 2), jnp.where(z == 0, 0, count - lax.div(z, 2)))


def copy_kernel(index_ref, states_ref, out_ref):
    out_ref[...] = states_ref[...]


def pick_kernel(slots, near, outer, index_ref, *refs):
    held, outs = refs[:outer], refs[outer:]
    block_z, seq = index_ref[2], index_ref[3]
    for s in range(slots):
        half = lax.rem(seq + slots - s, slots)
        for n in range(near):
            back = lax.rem(ring_place(block_z, outer) + outer - ring_place(half * near + n, outer), outer)
            for b in range(outer):

                @pl.when(back == b)
                def _():
                    outs[s][n] = held[b][...]


def join_kernel(index_ref, *refs):
    for s in range(len(refs) - 1):
        refs[-1][s] = refs[s][...]


def logits_kernel(docs, inner, strips, *refs):
    index_ref = refs[0]
    pieces = refs[1:1 + inner]
    heads = refs[1 + inner:1 + inner + strips]
    places_ref = refs[1 + inner + strips]
    logits_ref, rows_ref = refs[-2:]
    slots, near, _, part, width = pieces[0].shape
    length = slots * part

    @pl.when(pl.program_id(0) == 0)
    def _():
        for q in range(inner):
            lane_y = lax.rem(index_ref[0] + q, inner)
            for n in range(near):
                lane = pl.multiple_of((n * inner + lane_y) * width, width)
                for k in range(docs):
                    for s in range(slots):
                        rows_ref[pl.ds(k * length + s * part, part), pl.ds(lane, width)] = pieces[q][s, n, k]

    head = jnp.concatenate([ref[...] for ref in heads], axis=1)
    dense = lax.dot_general(
        rows_ref[...], head, (((1,), (1,)), ((), ())), preferred_element_type=jnp.float32
    )
    token = lax.broadcasted_iota(jnp.int32, (length, head.shape[0]), 0)
    for k in range(docs):
        picked = jnp.where(token == places_ref[pl.ds(k, 1), :], dense[k * length:(k + 1) * length], 0.0)
        logits_ref[pl.ds(k, 1), :] = jnp.sum(picked, axis=0, keepdims=True)


def hidden_kernel(docs, inner, strips, shape, *refs):
    index_ref = refs[0]
    heads = refs[1:1 + strips]
    places_ref, grads_ref = refs[1 + strips:3 + strips]
    outs = refs[3 + strips:3 + strips + inner]
    spread_ref, total_ref = refs[-2:]
    count, slots, near, _, part, width = shape
    length = slots * part
    step = pl.program_id(0)
    head = jnp.concatenate([ref[...] for ref in heads], axis=1)
    token = lax.broadcasted_iota(jnp.int32, (length, head.shape[0]), 0)
    for k in range(docs):
        spread = jnp.where(token == places_ref[pl.ds(k, 1), :], grads_ref[pl.ds(k, 1), :], 0.0)
        spread_ref[pl.ds(k * length, length), :] = spread.astype(jnp.bfloat16)
    term = jnp.dot(spread_ref[...], head, preferred_element_type=jnp.float32)

    @pl.when(step == 0)
    def _():
        total_ref[...] = term

    @pl.when(step > 0)
    def _():
        total_ref[...] += term

    @pl.when(step == pl.num_programs(0) - 1)
    def _():
        for q in range(inner):
            lane_y = lax.rem(index_ref[0] + q, inner)
            for i in range(count):
                for n in range(near):
                    lane = pl.multiple_of(((i * near + n) * inner + lane_y) * width, width)
                    for k in range(docs):
                        for s in range(slots):
                            piece = total_ref[pl.ds(k * length + s * part, part), pl.ds(lane, width)]
                            outs[q][i, s, n, k] = piece.astype(jnp.bfloat16)


def combine_kernel(inner, slots, index_ref, *refs):
    parts, outs = refs[:inner], refs[inner:]
    for i in range(parts[0].shape[0]):
        for s in range(slots):
            total = parts[0][i, s].astype(jnp.float32)
            for other in parts[1:]:
                total = total + other[i, s].astype(jnp.float32)
            outs[s][i] = total.astype(jnp.bfloat16)


def columns_kernel(groups, docs, index_ref, *refs):
    packed = refs[:groups]
    out_ref, turned_ref = refs[groups:]
    steps, _, columns = packed[0].shape
    count = groups * docs
    turned_ref[...] = jnp.zeros_like(turned_ref)
    for step in range(steps):
        for first in range(groups):

            @pl.when(index_ref[1] == first)
            def _():
                for g in range(groups):
                    place = (first + g) % groups * docs
                    turned_ref[place:place + docs, :columns] = packed[g][step, :docs]
                    turned_ref[count + place:count + place + docs, :columns] = packed[g][step, docs:2 * docs]

        turned = turned_ref[...].T
        out_ref[step * columns:(step + 1) * columns, :] = turned[:columns, :2 * count]


def sort_kernel(slots, near, outer, index_ref, *refs):
    mine, outs = refs[:slots], refs[slots:]
    block_z, seq = index_ref[2], index_ref[3]
    for ahead in range(outer):
        z = lax.rem(block_z + ahead, outer)
        slot = lax.rem(seq + slots - lax.div(z, near), slots)
        for s in range(slots):

            @pl.when(slot == s)
            def _():
                outs[ahead][...] = mine[s][:, lax.rem(z, near)]


def finish_kernel(counts, outer, index_ref, margin_ref, *refs):
    out_ref = refs[-1]
    docs = out_ref.shape[0]
    width = refs[0].shape[-1]
    c = 0
    for group, count in enumerate(counts):
        arrived = refs[group * outer:(group + 1) * outer]
        for i in range(count):
            for k in range(docs):
                total = arrived[0][i, k].astype(jnp.float32)
                for other in arrived[1:]:
                    total = total + other[i, k].astype(jnp.float32)
                out_ref[k, :, c * width:(c + 1) * width] = (total * margin_ref[k // 3]).astype(jnp.bfloat16)
            c += 1


def head_kernel(groups, docs, width, split, *refs):
    index_ref, margin_ref = refs[:2]
    rows = refs[2:2 + groups]
    columns_ref = refs[2 + groups]
    out_ref, token_ref, spread_ref = refs[-3 - split], refs[-2], refs[-1]
    chunks, tokens, lanes = rows[0].shape
    length = tokens // docs
    count = groups * docs

    @pl.when(pl.program_id(1) == 0)
    def _():
        token_ref[...] = jnp.zeros_like(token_ref)
        token = lax.broadcasted_iota(jnp.int32, (out_ref.shape[0], length), 1).astype(jnp.float32)
        for k in range(count):
            grads = columns_ref[:, k:k + 1] * margin_ref[k // 3]
            spread = jnp.where(token == columns_ref[:, count + k:count + k + 1], grads, 0.0)
            spread_ref[:, k * length:(k + 1) * length] = spread.astype(jnp.bfloat16)

    for first in range(groups):

        @pl.when(index_ref[1] == first)
        def _():
            total = None
            for g in range(groups):
                ref = rows[(g - first) % groups]
                features = jnp.concatenate(
                    [ref[c, :, lane:lane + width] for lane in range(0, lanes, width) for c in range(chunks)], axis=1
                )
                term = jnp.dot(
                    spread_ref[:, g * tokens:(g + 1) * tokens], features, preferred_element_type=jnp.float32
                )
                total = term if total is None else total + term
            if split:
                sent_ref = refs[-3]
                sent_ref[...] = total.astype(jnp.bfloat16)
                out_ref[...] = sent_ref[...].astype(jnp.float32)
            else:
                out_ref[...] = total


def widen_kernel(index_ref, piece_ref, previous_ref, out_ref, token_ref):
    token_ref[...] = jnp.zeros_like(token_ref)
    out_ref[...] = piece_ref[...].astype(jnp.float32)


def on_device(axes, hidden_states, head_weight, owner_pos, token_ids, teacher_margin):
    groups, slots, blocks = axes
    docs, part, block_width = hidden_states.shape
    depth, terms = head_weight.shape
    triples = teacher_margin.shape[0]
    inner = 2 if blocks % 2 == 0 else 1
    outer = blocks // inner
    near = outer // slots
    chunks = max(1, block_width // LANES)
    width = block_width // chunks
    length = slots * part
    tokens = docs * length
    columns = divisor(terms, 2048)
    steps = terms // columns
    strips = near * inner

    group = lax.axis_index("dp")
    seq = lax.axis_index("seq")
    block = lax.axis_index("vocab")
    block_y = lax.rem(block, inner)
    block_z = lax.div(block, inner)
    index = jnp.stack([block_y, group, block_z, seq]).astype(jnp.int32)

    def across_y(value, shift):
        perm = [(z * inner + y, z * inner + (y + shift) % inner) for z in range(outer) for y in range(inner)]
        return lax.ppermute(value, "vocab", perm)

    order = [0] + list(range(1, outer, 2)) + [z for z in range(outer - 1, 0, -1) if z % 2 == 0]

    def around_ring(value, steps_on):
        perm = [
            (order[p] * inner + y, order[(p + steps_on) % outer] * inner + y)
            for p in range(outer)
            for y in range(inner)
        ]
        return lax.ppermute(value, "vocab", perm)

    def across_z(value, shift):
        perm = [(z * inner + y, (z + shift) % outer * inner + y) for z in range(outer) for y in range(inner)]
        return lax.ppermute(value, "vocab", perm)

    def other_groups(value):
        return [value] + [lax.ppermute(value, "dp", shift_perm(groups, -g)) for g in range(1, groups)]

    def in_group_order(values):
        doubled = jnp.stack(values + values)
        return lax.dynamic_slice_in_dim(doubled, lax.rem(groups - group, groups), groups, axis=0)

    def blocked(value):
        return value.reshape(docs, steps, columns).transpose(1, 0, 2)

    head_rows = head_weight.T
    strip_specs = lambda c: [
        pl.BlockSpec((columns, width), functools.partial(lambda lane, v: (v, lane), strip * chunks + c))
        for strip in range(strips)
    ]
    row_spec = pl.BlockSpec((pl.squeezed, docs, columns), lambda v: (v, 0, 0))
    piece_shape = (slots, near, docs, part, width)
    piece_spec = pl.BlockSpec(piece_shape, lambda v: (0, 0, 0, 0, 0))
    index_spec = pl.BlockSpec(memory_space=pltpu.SMEM)
    vmem_spec = pl.BlockSpec(memory_space=pltpu.VMEM)
    any_spec = pl.BlockSpec(memory_space=pl.ANY)
    params = pltpu.CompilerParams(vmem_limit_bytes=VMEM_BYTES)

    def cost(flops, transferred):
        return pl.CostEstimate(flops=int(flops), bytes_accessed=int(transferred), transcendentals=0)

    owner_blocks = blocked(owner_pos)
    places = lax.rem(owner_blocks + (length - seq * part), length)
    own_lengths = jnp.sum((token_ids != 0).astype(jnp.int32), axis=1, keepdims=True)
    lengths = own_lengths
    for s in range(1, slots):
        lengths = lengths + lax.ppermute(own_lengths, "seq", shift_perm(slots, s))
    validity = (owner_blocks < lengths[None]).astype(jnp.float32)

    def run(kernel, name, operands, specs, shapes, out_specs=None, waits=(), flops=0, aliases={}, scratch=(), grid=(), prefetch=0):
        waits = [value for value in waits if value is not None]
        return pl.pallas_call(
            waiting(kernel, len(waits)),
            grid_spec=pltpu.PrefetchScalarGridSpec(
                num_scalar_prefetch=prefetch,
                grid=grid,
                in_specs=[index_spec] * (1 - prefetch) + [any_spec] * len(waits) + specs,
                out_specs=out_specs or [vmem_spec] * len(shapes),
                scratch_shapes=list(scratch),
            ),
            out_shape=shapes,
            input_output_aliases={1 + len(waits) + i: o for i, o in aliases.items()},
            compiler_params=params,
            cost_estimate=cost(flops, flops // 64),
            name=name,
        )(index, *waits, *operands)

    bf16 = lambda *shape: jax.ShapeDtypeStruct(shape, jnp.bfloat16)
    moved_shape = bf16(near, docs, part, width)
    sliced = [hidden_states[:, :, c * width:(c + 1) * width] for c in range(chunks)]
    last = chunks - 1
    gathered_chunks = []
    others = []
    logit_parts = []
    features = None

    def add_logits(c, waits):
        nonlocal features
        previous = [] if features is None else [features]
        chunk_logits, features = run(
            functools.partial(logits_kernel, docs, inner, strips),
            "pooled_logits",
            [gathered_chunks[c], others[c]][:inner] + [head_rows] * strips + [places, *previous],
            [piece_spec] * inner + strip_specs(c) + [row_spec] + [any_spec] * len(previous),
            [
                jax.ShapeDtypeStruct((steps, docs, columns), jnp.float32),
                bf16(chunks, tokens, strips * width),
            ],
            out_specs=[
                row_spec,
                pl.BlockSpec(
                    (pl.squeezed, tokens, strips * width), functools.partial(lambda c, v: (c, 0, 0), c)
                ),
            ],
            waits=waits,
            flops=2 * tokens * strips * width * terms,
            aliases={inner + strips + 1: 1} if previous else {},
            grid=(steps,),
        )
        logit_parts.append(chunk_logits)

    first_step = None
    picked = []
    for c in range(chunks):
        own = sliced[c]
        if c > 0:
            (own,) = run(
                copy_kernel,
                "feature_chunk",
                [own],
                [vmem_spec],
                [bf16(docs, part, width)],
                waits=[first_step, picked[c - 2] if c > 1 else None],
            )
        held = [own]
        for back in range(1, outer):
            held.append(around_ring(own, back) if c == 0 else around_ring(held[-1], 1))
        first_step = held[min(1, outer - 1)]
        mine, *sends = run(
            functools.partial(pick_kernel, slots, near, outer),
            "pick_halves",
            held,
            [vmem_spec] * outer,
            [moved_shape] * slots,
            waits=[gathered_chunks[c - 1] if c > 0 else None],
        )
        picked.append(mine)
        arrived = [lax.ppermute(sends[s - 1], "seq", shift_perm(slots, -s)) for s in range(1, slots)]
        if c == last and c > 1:
            add_logits(0, [mine])
        (gathered,) = run(
            join_kernel,
            "join_tokens",
            [mine, *arrived],
            [vmem_spec] * slots,
            [bf16(*piece_shape)],
            waits=[others[c - 2] if c > 1 else None, logit_parts[0] if logit_parts else None],
        )
        gathered_chunks.append(gathered)
        others.append(across_y(gathered, -1) if inner > 1 else None)
    for c in range(len(logit_parts), chunks):
        add_logits(c, [validity, others[-2]] if c == 1 else [])

    logit_part = functools.reduce(jnp.add, logit_parts)
    logits = logit_part
    for s in range(1, slots):
        logits = logits + lax.ppermute(logit_part, "seq", shift_perm(slots, s))
    softened = jax.nn.softplus(logits)
    pooled = validity * jnp.log1p(softened)
    slopes = validity * jax.nn.sigmoid(logits) / (1.0 + softened)
    view = pooled.reshape(steps, triples, 3, columns)
    query, positive, negative = view[:, :, 0], view[:, :, 1], view[:, :, 2]
    unscaled = jnp.stack([positive - negative, query, -query], axis=2).reshape(logits.shape) * slopes
    unscaled = unscaled.astype(jnp.bfloat16)
    unscaled = unscaled.astype(jnp.float32)
    scores = jnp.sum(query * positive, axis=(0, 2)) - jnp.sum(query * negative, axis=(0, 2))
    paired = blocks & (blocks - 1) == 0
    distance = 1

    def add_distance(value, distance):
        return value + lax.ppermute(value, "vocab", [(i, i ^ distance) for i in range(blocks)])

    if paired and blocks > 1:
        scores = add_distance(scores, distance)
        distance *= 2
    score_row = jnp.pad(jnp.concatenate([scores, teacher_margin]), (0, columns - 2 * triples))
    packed = jnp.concatenate(
        [unscaled, places.astype(jnp.float32), jnp.broadcast_to(score_row, (steps, 1, columns))], axis=1
    )
    packed_all = other_groups(packed)
    scores = in_group_order([scores] + [value[0, 2 * docs, :triples] for value in packed_all[1:]])
    teacher = in_group_order([teacher_margin] + [value[0, 2 * docs, triples:2 * triples] for value in packed_all[1:]])
    if paired:
        while distance < blocks:
            scores = add_distance(scores, distance)
            distance *= 2
    else:
        scores = lax.psum(scores, "vocab")
    margin_all = ((scores - teacher) / (triples * groups)).reshape(-1)
    margin = lax.dynamic_slice(margin_all, (group * triples,), (triples,))
    (head_columns,) = run(
        functools.partial(columns_kernel, groups, docs),
        "turn_gradients",
        packed_all,
        [vmem_spec] * groups,
        [jax.ShapeDtypeStruct((terms, 2 * groups * docs), jnp.float32)],
        scratch=[pltpu.VMEM((-(-2 * groups * docs // 8) * 8, -(-columns // LANES) * LANES), jnp.float32)],
    )
    features_all = other_groups(features)

    head_terms = divisor(terms, 800)
    ranges = terms // head_terms
    owned = (ranges - 1) // groups if groups > 1 else 0
    grad_head = token = None
    shares = []

    def run_head(start, count, split, *waits):
        nonlocal grad_head, token
        if count == 0:
            return
        previous = [] if grad_head is None else [grad_head]
        row = lambda r, index_ref: start + r + (index_ref[1] * owned if split else 0)
        grad_head, *sent, token = run(
            functools.partial(head_kernel, groups, docs, width, split),
            "head_terms",
            [margin_all, *features_all, head_columns, *previous],
            [index_spec]
            + [pl.BlockSpec((chunks, tokens, width), lambda r, d, index_ref: (0, 0, d))] * groups
            + [pl.BlockSpec((head_terms, 2 * groups * docs), lambda r, d, index_ref: (row(r, index_ref), 0))]
            + [any_spec] * len(previous),
            [jax.ShapeDtypeStruct((terms, depth), jnp.float32)]
            + [bf16(count * head_terms, depth)] * split
            + [jax.ShapeDtypeStruct((8, LANES), jnp.float32)],
            out_specs=[pl.BlockSpec((head_terms, block_width), lambda r, d, index_ref: (row(r, index_ref), d))]
            + [pl.BlockSpec((head_terms, block_width), lambda r, d, index_ref: (r, d))] * split
            + [pl.BlockSpec((8, LANES), lambda r, d, index_ref: (0, 0))],
            waits=waits,
            flops=count * 2 * groups * tokens * head_terms * depth * (1 if split else 1024) // 4,
            aliases={2 + groups: 0} if previous else {},
            scratch=[pltpu.VMEM((head_terms, groups * tokens), jnp.bfloat16)],
            grid=(count, strips),
            prefetch=1,
        )
        if split:
            shares.append((start, other_groups(sent[0])[1:]))

    def widen_shares():
        nonlocal grad_head, token
        for start, arrived in shares:
            for g, piece in enumerate(arrived, 1):

                def row(r, index_ref, start=start, g=g):
                    return start + r + lax.rem(index_ref[1] + g, groups) * owned

                grad_head, token = run(
                    widen_kernel,
                    "widen_share",
                    [piece, grad_head],
                    [pl.BlockSpec((head_terms // 2, depth), lambda r, index_ref: (r, 0)), any_spec],
                    [
                        jax.ShapeDtypeStruct((terms, depth), jnp.float32),
                        jax.ShapeDtypeStruct((8, LANES), jnp.float32),
                    ],
                    out_specs=[
                        pl.BlockSpec(
                            (head_terms // 2, depth),
                            functools.partial(lambda row, r, index_ref: (2 * row(0, index_ref) + r, 0), row),
                        ),
                        pl.BlockSpec((8, LANES), lambda r, index_ref: (0, 0)),
                    ],
                    flops=piece.size,
                    aliases={1: 0},
                    grid=(2 * piece.shape[0] // head_terms,),
                    prefetch=1,
                )

    half = -(-chunks // 2)
    chunk_groups = [members for members in (range(half), range(half, chunks)) if members]
    pairs = []
    for members in chunk_groups:
        pair_shape = (len(members), *piece_shape)
        lanes = len(members) * strips * width
        sums = run(
            functools.partial(hidden_kernel, docs, inner, len(members) * strips, pair_shape),
            "hidden_terms",
            [head_rows] * (len(members) * strips) + [places, unscaled],
            [spec for c in members for spec in strip_specs(c)] + [row_spec, row_spec],
            [bf16(*pair_shape)] * inner,
            out_specs=[pl.BlockSpec(pair_shape, lambda v: (0,) * 6)] * inner,
            waits=[packed] if pairs else [],
            flops=2 * tokens * lanes * terms // 4,
            scratch=[pltpu.VMEM((tokens, columns), jnp.bfloat16), pltpu.VMEM((tokens, lanes), jnp.float32)],
            grid=(steps,),
        )
        pairs.append([sums[0]] + [across_y(sums[q], q) for q in range(1, inner)])

    mine_all = []
    arrived_all = []

    def add_blocks(pair, *waits):
        count = pair[0].shape[0]
        mine = run(
            functools.partial(combine_kernel, inner, slots),
            "add_blocks",
            pair,
            [vmem_spec] * inner,
            [bf16(count, near, docs, part, width)] * slots,
            waits=waits,
        )
        mine_all.append([mine[0]] + [lax.ppermute(mine[s], "seq", shift_perm(slots, s)) for s in range(1, slots)])

    def sort_pieces(mine, *waits):
        pieces = run(
            functools.partial(sort_kernel, slots, near, outer),
            "sort_pieces",
            mine,
            [vmem_spec] * slots,
            [bf16(mine[0].shape[0], docs, part, width)] * outer,
            waits=waits,
        )
        arrived_all.append([pieces[0]] + [across_z(pieces[ahead], ahead) for ahead in range(1, outer)])

    early = -(-owned // 2)
    add_blocks(pairs[0])
    run_head(0, early, True, mine_all[0][0], pairs[-1][0])
    sort_pieces(mine_all[0], token)
    if len(pairs) > 1:
        add_blocks(pairs[1], arrived_all[0][0])
    run_head(early, owned - early, True, arrived_all[0][0], mine_all[-1][0])
    if len(pairs) > 1:
        sort_pieces(mine_all[1], token)
    run_head(owned * groups, ranges - owned * groups, False, arrived_all[-1][0], *arrived_all[0][1:])
    widen_shares()
    (grad_hidden,) = run(
        functools.partial(finish_kernel, [len(members) for members in chunk_groups], outer),
        "scale_hidden",
        [margin] + [value for arrived in arrived_all for value in arrived],
        [index_spec] + [vmem_spec] * (len(pairs) * outer),
        [bf16(docs, part, block_width)],
        waits=[token],
    )
    return (grad_head.T, grad_hidden)


def solution(mesh):
    axes = (mesh.shape["dp"], mesh.shape["seq"], mesh.shape["vocab"])
    return jax.shard_map(
        functools.partial(on_device, axes),
        mesh=mesh,
        in_specs=(
            P("dp", "seq", "vocab"),
            P("seq", "vocab"),
            P("dp", "vocab"),
            P("dp", "seq"),
            P("dp"),
        ),
        out_specs=(P("seq", "vocab"), P("dp", "seq", "vocab")),
        check_vma=False,
    )
```

```python
import functools

import jax
import jax.numpy as jnp
from jax import lax
from jax.experimental import pallas as pl
from jax.experimental.pallas import tpu as pltpu
from jax.sharding import PartitionSpec as P

LANES = 128
VMEM_BYTES = 48 * 1024 * 1024
HEAD_VMEM_BYTES = 58 * 1024 * 1024


def shift_perm(count, shift):
    return [(i, (i + shift) % count) for i in range(count)]


def waiting(kernel, count):
    return lambda *refs: kernel(refs[0], *refs[1 + count:])


def marking(kernel, scratch):
    def marked(*refs):
        at = len(refs) - 1 - scratch
        refs[at][...] = jnp.zeros_like(refs[at])
        kernel(*refs[:at], *refs[at + 1:])

    return marked


def divisor(terms, limit):
    fits = [b for b in range(16, limit + 1, 16) if terms % b == 0]
    return fits[-1] if fits else terms


def ring_place(z, count):
    return jnp.where(lax.rem(z, 2) == 1, lax.div(z + 1, 2), jnp.where(z == 0, 0, count - lax.div(z, 2)))


def copy_kernel(index_ref, states_ref, out_ref):
    out_ref[...] = states_ref[...]


def pick_kernel(slots, near, outer, index_ref, *refs):
    held, outs = refs[:outer], refs[outer:]
    block_z, seq = index_ref[2], index_ref[3]
    for s in range(slots):
        half = lax.rem(seq + slots - s, slots)
        for n in range(near):
            back = lax.rem(ring_place(block_z, outer) + outer - ring_place(half * near + n, outer), outer)
            for b in range(outer):

                @pl.when(back == b)
                def _():
                    outs[s][n] = held[b][...]


def join_kernel(index_ref, *refs):
    for s in range(len(refs) - 1):
        refs[-1][s] = refs[s][...]


def logits_kernel(docs, inner, strips, *refs):
    index_ref = refs[0]
    pieces = refs[1:1 + inner]
    heads = refs[1 + inner:1 + inner + strips]
    places_ref = refs[1 + inner + strips]
    logits_ref, rows_ref = refs[-2:]
    slots, near, _, part, width = pieces[0].shape
    length = slots * part

    @pl.when(pl.program_id(0) == 0)
    def _():
        for q in range(inner):
            lane_y = lax.rem(index_ref[0] + q, inner)
            for n in range(near):
                lane = pl.multiple_of((n * inner + lane_y) * width, width)
                for k in range(docs):
                    for s in range(slots):
                        rows_ref[pl.ds(k * length + s * part, part), pl.ds(lane, width)] = pieces[q][s, n, k]

    head = jnp.concatenate([ref[...] for ref in heads], axis=1)
    dense = lax.dot_general(
        rows_ref[...], head, (((1,), (1,)), ((), ())), preferred_element_type=jnp.float32
    )
    token = lax.broadcasted_iota(jnp.int32, (length, head.shape[0]), 0)
    for k in range(docs):
        picked = jnp.where(token == places_ref[pl.ds(k, 1), :], dense[k * length:(k + 1) * length], 0.0)
        logits_ref[pl.ds(k, 1), :] = jnp.sum(picked, axis=0, keepdims=True)


def hidden_kernel(docs, inner, strips, shape, *refs):
    index_ref = refs[0]
    heads = refs[1:1 + strips]
    places_ref, grads_ref = refs[1 + strips:3 + strips]
    outs = refs[3 + strips:3 + strips + inner]
    spread_ref, total_ref = refs[-2:]
    count, slots, near, _, part, width = shape
    length = slots * part
    step = pl.program_id(0)
    head = jnp.concatenate([ref[...] for ref in heads], axis=1)
    token = lax.broadcasted_iota(jnp.int32, (length, head.shape[0]), 0)
    for k in range(docs):
        spread = jnp.where(token == places_ref[pl.ds(k, 1), :], grads_ref[pl.ds(k, 1), :], 0.0)
        spread_ref[pl.ds(k * length, length), :] = spread.astype(jnp.bfloat16)
    term = jnp.dot(spread_ref[...], head, preferred_element_type=jnp.float32)

    @pl.when(step == 0)
    def _():
        total_ref[...] = term

    @pl.when(step > 0)
    def _():
        total_ref[...] += term

    @pl.when(step == pl.num_programs(0) - 1)
    def _():
        for q in range(inner):
            lane_y = lax.rem(index_ref[0] + q, inner)
            for i in range(count):
                for n in range(near):
                    lane = pl.multiple_of(((i * near + n) * inner + lane_y) * width, width)
                    for k in range(docs):
                        for s in range(slots):
                            piece = total_ref[pl.ds(k * length + s * part, part), pl.ds(lane, width)]
                            outs[q][i, s, n, k] = piece.astype(jnp.bfloat16)


def combine_kernel(inner, slots, index_ref, *refs):
    parts, outs = refs[:inner], refs[inner:]
    for i in range(parts[0].shape[0]):
        for s in range(slots):
            total = parts[0][i, s].astype(jnp.float32)
            for other in parts[1:]:
                total = total + other[i, s].astype(jnp.float32)
            outs[s][i] = total.astype(jnp.bfloat16)


def columns_kernel(groups, docs, index_ref, *refs):
    packed = refs[:groups]
    out_ref, turned_ref = refs[groups:]
    steps, _, columns = packed[0].shape
    count = groups * docs
    turned_ref[...] = jnp.zeros_like(turned_ref)
    for step in range(steps):
        for first in range(groups):

            @pl.when(index_ref[1] == first)
            def _():
                for g in range(groups):
                    place = (first + g) % groups * docs
                    turned_ref[place:place + docs, :columns] = packed[g][step, :docs]
                    turned_ref[count + place:count + place + docs, :columns] = packed[g][step, docs:2 * docs]

        turned = turned_ref[...].T
        out_ref[step * columns:(step + 1) * columns, :] = turned[:columns, :2 * count]


def sort_kernel(slots, near, outer, index_ref, *refs):
    mine, outs = refs[:slots], refs[slots:]
    block_z, seq = index_ref[2], index_ref[3]
    for ahead in range(outer):
        z = lax.rem(block_z + ahead, outer)
        slot = lax.rem(seq + slots - lax.div(z, near), slots)
        for s in range(slots):

            @pl.when(slot == s)
            def _():
                outs[ahead][...] = mine[s][:, lax.rem(z, near)]


def finish_kernel(counts, outer, index_ref, margin_ref, *refs):
    out_ref = refs[-1]
    docs = out_ref.shape[0]
    width = refs[0].shape[-1]
    c = 0
    for group, count in enumerate(counts):
        arrived = refs[group * outer:(group + 1) * outer]
        for i in range(count):
            for k in range(docs):
                total = arrived[0][i, k].astype(jnp.float32)
                for other in arrived[1:]:
                    total = total + other[i, k].astype(jnp.float32)
                out_ref[k, :, c * width:(c + 1) * width] = (total * margin_ref[k // 3]).astype(jnp.bfloat16)
            c += 1


def head_kernel(groups, docs, *refs):
    index_ref, margin_ref = refs[:2]
    rows = refs[2:2 + groups]
    columns_ref = refs[2 + groups]
    out_ref, token_ref, spread_ref = refs[-3:]
    chunks, tokens, width = rows[0].shape
    length = tokens // docs
    count = groups * docs

    @pl.when(pl.program_id(1) == 0)
    def _():
        token_ref[...] = jnp.zeros_like(token_ref)
        token = lax.broadcasted_iota(jnp.int32, (out_ref.shape[0], length), 1).astype(jnp.float32)
        for k in range(count):
            grads = columns_ref[:, k:k + 1] * margin_ref[k // 3]
            spread = jnp.where(token == columns_ref[:, count + k:count + k + 1], grads, 0.0)
            spread_ref[:, k * length:(k + 1) * length] = spread.astype(jnp.bfloat16)

    for first in range(groups):

        @pl.when(index_ref[1] == first)
        def _():
            total = None
            for g in range(groups):
                ref = rows[(g - first) % groups]
                features = jnp.concatenate([ref[c] for c in range(chunks)], axis=1)
                term = jnp.dot(
                    spread_ref[:, g * tokens:(g + 1) * tokens], features, preferred_element_type=jnp.float32
                )
                total = term if total is None else total + term
            out_ref[...] = total


def on_device(axes, hidden_states, head_weight, owner_pos, token_ids, teacher_margin):
    groups, slots, blocks = axes
    docs, part, block_width = hidden_states.shape
    depth, terms = head_weight.shape
    triples = teacher_margin.shape[0]
    inner = 2 if blocks % 2 == 0 else 1
    outer = blocks // inner
    near = outer // slots
    chunks = max(1, block_width // LANES)
    width = block_width // chunks
    length = slots * part
    tokens = docs * length
    columns = divisor(terms, 2048)
    steps = terms // columns
    strips = near * inner

    group = lax.axis_index("dp")
    seq = lax.axis_index("seq")
    block = lax.axis_index("vocab")
    block_y = lax.rem(block, inner)
    block_z = lax.div(block, inner)
    index = jnp.stack([block_y, group, block_z, seq]).astype(jnp.int32)

    def across_y(value, shift):
        perm = [(z * inner + y, z * inner + (y + shift) % inner) for z in range(outer) for y in range(inner)]
        return lax.ppermute(value, "vocab", perm)

    order = [0] + list(range(1, outer, 2)) + [z for z in range(outer - 1, 0, -1) if z % 2 == 0]

    def around_ring(value, steps_on):
        perm = [
            (order[p] * inner + y, order[(p + steps_on) % outer] * inner + y)
            for p in range(outer)
            for y in range(inner)
        ]
        return lax.ppermute(value, "vocab", perm)

    def across_z(value, shift):
        perm = [(z * inner + y, (z + shift) % outer * inner + y) for z in range(outer) for y in range(inner)]
        return lax.ppermute(value, "vocab", perm)

    def other_groups(value):
        return [value] + [lax.ppermute(value, "dp", shift_perm(groups, -g)) for g in range(1, groups)]

    def in_group_order(values):
        doubled = jnp.stack(values + values)
        return lax.dynamic_slice_in_dim(doubled, lax.rem(groups - group, groups), groups, axis=0)

    def blocked(value):
        return value.reshape(docs, steps, columns).transpose(1, 0, 2)

    head_rows = head_weight.T
    strip_specs = lambda c: [
        pl.BlockSpec((columns, width), functools.partial(lambda lane, v: (v, lane), strip * chunks + c))
        for strip in range(strips)
    ]
    row_spec = pl.BlockSpec((pl.squeezed, docs, columns), lambda v: (v, 0, 0))
    piece_shape = (slots, near, docs, part, width)
    piece_spec = pl.BlockSpec(piece_shape, lambda v: (0, 0, 0, 0, 0))
    index_spec = pl.BlockSpec(memory_space=pltpu.SMEM)
    vmem_spec = pl.BlockSpec(memory_space=pltpu.VMEM)
    any_spec = pl.BlockSpec(memory_space=pl.ANY)

    def cost(flops, transferred):
        return pl.CostEstimate(flops=int(flops), bytes_accessed=int(transferred), transcendentals=0)

    owner_blocks = blocked(owner_pos)
    places = lax.rem(owner_blocks + (length - seq * part), length)
    own_lengths = jnp.sum((token_ids != 0).astype(jnp.float32), axis=1)

    def run(
        kernel, name, operands, specs, shapes, out_specs=None, waits=(), flops=0, aliases={}, scratch=(), grid=(),
        mark=False, limit=VMEM_BYTES,
    ):
        waits = [value for value in waits if value is not None]
        out_specs = list(out_specs or [vmem_spec] * len(shapes))
        if mark:
            kernel = marking(kernel, len(scratch))
            shapes = list(shapes) + [jax.ShapeDtypeStruct((8, LANES), jnp.float32)]
            out_specs.append(pl.BlockSpec((8, LANES), lambda *_: (0, 0)) if grid else vmem_spec)
        return pl.pallas_call(
            waiting(kernel, len(waits)),
            grid=grid,
            in_specs=[index_spec] + [any_spec] * len(waits) + specs,
            out_specs=out_specs,
            out_shape=shapes,
            scratch_shapes=list(scratch),
            input_output_aliases={1 + len(waits) + i: o for i, o in aliases.items()},
            compiler_params=pltpu.CompilerParams(vmem_limit_bytes=limit),
            cost_estimate=cost(flops, flops // 64),
            name=name,
        )(index, *waits, *operands)

    bf16 = lambda *shape: jax.ShapeDtypeStruct(shape, jnp.bfloat16)
    moved_shape = bf16(near, docs, part, width)
    sliced = [hidden_states[:, :, c * width:(c + 1) * width] for c in range(chunks)]
    last = chunks - 1
    gathered_chunks = []
    others = []
    logit_parts = []
    features = None

    def add_logits(c, waits):
        nonlocal features
        previous = [] if features is None else [features]
        chunk_logits, features = run(
            functools.partial(logits_kernel, docs, inner, strips),
            "pooled_logits",
            [gathered_chunks[c], others[c]][:inner] + [head_rows] * strips + [places, *previous],
            [piece_spec] * inner + strip_specs(c) + [row_spec] + [any_spec] * len(previous),
            [
                jax.ShapeDtypeStruct((steps, docs, columns), jnp.float32),
                bf16(chunks, tokens, strips * width),
            ],
            out_specs=[
                row_spec,
                pl.BlockSpec(
                    (pl.squeezed, tokens, strips * width), functools.partial(lambda c, v: (c, 0, 0), c)
                ),
            ],
            waits=waits,
            flops=2 * tokens * strips * width * terms,
            aliases={inner + strips + 1: 1} if previous else {},
            grid=(steps,),
        )
        logit_parts.append(chunk_logits)

    first_step = None
    for c in range(chunks):
        own = sliced[c]
        if c > 0:
            (own,) = run(
                copy_kernel, "feature_chunk", [own], [vmem_spec], [bf16(docs, part, width)], waits=[first_step]
            )
        held = [own]
        for back in range(1, outer):
            held.append(around_ring(own, back) if c == 0 else around_ring(held[-1], 1))
        first_step = held[min(1, outer - 1)]
        mine, *sends = run(
            functools.partial(pick_kernel, slots, near, outer),
            "pick_halves",
            held,
            [vmem_spec] * outer,
            [moved_shape] * slots,
            waits=[gathered_chunks[c - 1] if c > 0 else None, others[c - 2] if c > 1 else None],
        )
        arrived = [lax.ppermute(sends[s - 1], "seq", shift_perm(slots, -s)) for s in range(1, slots)]
        if c == last and c > 1:
            add_logits(0, [mine])
        (gathered,) = run(
            join_kernel,
            "join_tokens",
            [mine, *arrived],
            [vmem_spec] * slots,
            [bf16(*piece_shape)],
            waits=[others[c - 2] if c > 1 else None, logit_parts[0] if logit_parts else None],
        )
        gathered_chunks.append(gathered)
        others.append(across_y(gathered, -1) if inner > 1 else None)
    for c in range(len(logit_parts), chunks):
        add_logits(c, [others[-2]] if c == 1 else [])

    logits = functools.reduce(jnp.add, logit_parts)
    lengths = own_lengths
    length_row = jnp.broadcast_to(jnp.pad(own_lengths, (0, columns - docs)).reshape(1, 1, columns), (steps, 1, columns))
    counted = jnp.concatenate([logits, length_row], axis=1)
    for s in range(1, slots):
        arrived = lax.ppermute(counted, "seq", shift_perm(slots, s))
        logits = logits + arrived[:, :docs]
        lengths = lengths + arrived[0, docs, :docs]
    validity = (owner_blocks < lengths[None, :, None].astype(jnp.int32)).astype(jnp.float32)
    softened = jax.nn.softplus(logits)
    pooled = validity * jnp.log1p(softened)
    slopes = validity * jax.nn.sigmoid(logits) / (1.0 + softened)
    view = pooled.reshape(steps, triples, 3, columns)
    query, positive, negative = view[:, :, 0], view[:, :, 1], view[:, :, 2]
    unscaled = jnp.stack([positive - negative, query, -query], axis=2).reshape(logits.shape) * slopes
    unscaled = unscaled.astype(jnp.bfloat16)
    unscaled = unscaled.astype(jnp.float32)
    scores = jnp.sum(query * positive, axis=(0, 2)) - jnp.sum(query * negative, axis=(0, 2))
    paired = blocks & (blocks - 1) == 0
    distance = 1

    def add_distance(value, distance):
        return value + lax.ppermute(value, "vocab", [(i, i ^ distance) for i in range(blocks)])

    if paired and blocks > 1:
        scores = add_distance(scores, distance)
        distance *= 2
    score_row = jnp.pad(jnp.concatenate([scores, teacher_margin]), (0, columns - 2 * triples))
    packed = jnp.concatenate(
        [unscaled, places.astype(jnp.float32), jnp.broadcast_to(score_row, (steps, 1, columns))], axis=1
    )
    packed_all = other_groups(packed)
    scores = in_group_order([scores] + [value[0, 2 * docs, :triples] for value in packed_all[1:]])
    teacher = in_group_order([teacher_margin] + [value[0, 2 * docs, triples:2 * triples] for value in packed_all[1:]])
    if paired:
        while distance < blocks:
            scores = add_distance(scores, distance)
            distance *= 2
    else:
        scores = lax.psum(scores, "vocab")
    margin_all = ((scores - teacher) / (triples * groups)).reshape(-1)
    margin = lax.dynamic_slice(margin_all, (group * triples,), (triples,))
    (head_columns,) = run(
        functools.partial(columns_kernel, groups, docs),
        "turn_gradients",
        packed_all,
        [vmem_spec] * groups,
        [jax.ShapeDtypeStruct((terms, 2 * groups * docs), jnp.float32)],
        scratch=[pltpu.VMEM((-(-2 * groups * docs // 8) * 8, -(-columns // LANES) * LANES), jnp.float32)],
    )
    features_all = other_groups(features)

    head_terms = divisor(terms, 800)
    ranges = terms // head_terms
    next_range = 0
    grad_head = token = None

    def run_head(count, *waits):
        nonlocal grad_head, token, next_range
        if count == 0:
            return
        previous = [] if grad_head is None else [grad_head]
        start = next_range
        term_spec = pl.BlockSpec((head_terms, 2 * groups * docs), lambda r, d: (start + r, 0))
        grad_head, token = run(
            functools.partial(head_kernel, groups, docs),
            "head_terms",
            [margin_all, *features_all, head_columns, *previous],
            [index_spec]
            + [pl.BlockSpec((chunks, tokens, width), lambda r, d: (0, 0, d))] * groups
            + [term_spec]
            + [any_spec] * len(previous),
            [jax.ShapeDtypeStruct((terms, depth), jnp.float32), jax.ShapeDtypeStruct((8, LANES), jnp.float32)],
            out_specs=[
                pl.BlockSpec((head_terms, block_width), lambda r, d: (start + r, d)),
                pl.BlockSpec((8, LANES), lambda r, d: (0, 0)),
            ],
            waits=waits,
            flops=count * 2 * groups * tokens * head_terms * depth // 4,
            aliases={2 + groups: 0} if previous else {},
            scratch=[pltpu.VMEM((head_terms, groups * tokens), jnp.bfloat16)],
            grid=(count, strips),
            limit=HEAD_VMEM_BYTES,
        )
        next_range += count

    half = -(-chunks // 2)
    chunk_groups = [members for members in (range(half), range(half, chunks)) if members]
    pairs = []
    marks = []
    for members in chunk_groups:
        pair_shape = (len(members), *piece_shape)
        lanes = len(members) * strips * width
        *sums, mark = run(
            functools.partial(hidden_kernel, docs, inner, len(members) * strips, pair_shape),
            "hidden_terms",
            [head_rows] * (len(members) * strips) + [places, unscaled],
            [spec for c in members for spec in strip_specs(c)] + [row_spec, row_spec],
            [bf16(*pair_shape)] * inner,
            out_specs=[pl.BlockSpec(pair_shape, lambda v: (0,) * 6)] * inner,
            waits=[packed] if pairs else [],
            mark=True,
            flops=2 * tokens * lanes * terms // 4,
            scratch=[pltpu.VMEM((tokens, columns), jnp.bfloat16), pltpu.VMEM((tokens, lanes), jnp.float32)],
            grid=(steps,),
        )
        marks.append(mark)
        pairs.append([sums[0]] + [across_y(sums[q], q) for q in range(1, inner)])

    share = ranges // 5
    mine_all = []
    arrived_all = []

    def add_blocks(pair, *waits):
        count = pair[0].shape[0]
        *mine, mark = run(
            functools.partial(combine_kernel, inner, slots),
            "add_blocks",
            pair,
            [vmem_spec] * inner,
            [bf16(count, near, docs, part, width)] * slots,
            waits=waits,
            mark=True,
        )
        mine_all.append([mine[0]] + [lax.ppermute(mine[s], "seq", shift_perm(slots, s)) for s in range(1, slots)])
        return mark

    def sort_pieces(mine, *waits):
        *pieces, mark = run(
            functools.partial(sort_kernel, slots, near, outer),
            "sort_pieces",
            mine,
            [vmem_spec] * slots,
            [bf16(mine[0].shape[0], docs, part, width)] * outer,
            waits=waits,
            mark=True,
        )
        arrived_all.append([pieces[0]] + [across_z(pieces[ahead], ahead) for ahead in range(1, outer)])
        return mark

    added = add_blocks(pairs[0])
    run_head(2 * share, added, marks[-1])
    sorted_mark = sort_pieces(mine_all[0], token)
    if len(pairs) > 1:
        added = add_blocks(pairs[1], sorted_mark)
        run_head(share, sorted_mark, added)
        sorted_mark = sort_pieces(mine_all[1], token)
    run_head(ranges - next_range, sorted_mark)
    (grad_hidden,) = run(
        functools.partial(finish_kernel, [len(members) for members in chunk_groups], outer),
        "scale_hidden",
        [margin] + [value for arrived in arrived_all for value in arrived],
        [index_spec] + [vmem_spec] * (len(pairs) * outer),
        [bf16(docs, part, block_width)],
        waits=[token],
    )
    return (grad_head.T, grad_hidden)


def solution(mesh):
    axes = (mesh.shape["dp"], mesh.shape["seq"], mesh.shape["vocab"])
    return jax.shard_map(
        functools.partial(on_device, axes),
        mesh=mesh,
        in_specs=(
            P("dp", "seq", "vocab"),
            P("seq", "vocab"),
            P("dp", "vocab"),
            P("dp", "seq"),
            P("dp"),
        ),
        out_specs=(P("seq", "vocab"), P("dp", "seq", "vocab")),
        check_vma=False,
    )
```

```python
import functools

import jax
import jax.numpy as jnp
from jax import lax
from jax.experimental import pallas as pl
from jax.experimental.pallas import tpu as pltpu
from jax.sharding import PartitionSpec as P

LANES = 128
VMEM_BYTES = 48 * 1024 * 1024
HEAD_VMEM_BYTES = 58 * 1024 * 1024


def shift_perm(count, shift):
    return [(i, (i + shift) % count) for i in range(count)]


def waiting(kernel, count):
    return lambda *refs: kernel(refs[0], *refs[1 + count:])


def divisor(terms, limit):
    fits = [b for b in range(16, limit + 1, 16) if terms % b == 0]
    return fits[-1] if fits else terms


def ring_place(z, count):
    return jnp.where(lax.rem(z, 2) == 1, lax.div(z + 1, 2), jnp.where(z == 0, 0, count - lax.div(z, 2)))


def copy_kernel(index_ref, states_ref, out_ref):
    out_ref[...] = states_ref[...]


def pick_kernel(slots, near, outer, index_ref, *refs):
    held, outs = refs[:outer], refs[outer:]
    block_z, seq = index_ref[2], index_ref[3]
    for s in range(slots):
        half = lax.rem(seq + slots - s, slots)
        for n in range(near):
            back = lax.rem(ring_place(block_z, outer) + outer - ring_place(half * near + n, outer), outer)
            for b in range(outer):

                @pl.when(back == b)
                def _():
                    outs[s][n] = held[b][...]


def join_kernel(index_ref, *refs):
    for s in range(len(refs) - 1):
        refs[-1][s] = refs[s][...]


def logits_kernel(docs, inner, strips, *refs):
    index_ref = refs[0]
    pieces = refs[1:1 + inner]
    heads = refs[1 + inner:1 + inner + strips]
    places_ref = refs[1 + inner + strips]
    logits_ref, rows_ref = refs[-2:]
    slots, near, _, part, width = pieces[0].shape
    length = slots * part

    @pl.when(pl.program_id(0) == 0)
    def _():
        for q in range(inner):
            lane_y = lax.rem(index_ref[0] + q, inner)
            for n in range(near):
                lane = pl.multiple_of((n * inner + lane_y) * width, width)
                for k in range(docs):
                    for s in range(slots):
                        rows_ref[pl.ds(k * length + s * part, part), pl.ds(lane, width)] = pieces[q][s, n, k]

    head = jnp.concatenate([ref[...] for ref in heads], axis=1)
    dense = lax.dot_general(
        rows_ref[...], head, (((1,), (1,)), ((), ())), preferred_element_type=jnp.float32
    )
    token = lax.broadcasted_iota(jnp.int32, (length, head.shape[0]), 0)
    for k in range(docs):
        picked = jnp.where(token == places_ref[pl.ds(k, 1), :], dense[k * length:(k + 1) * length], 0.0)
        logits_ref[pl.ds(k, 1), :] = jnp.sum(picked, axis=0, keepdims=True)


def hidden_kernel(docs, inner, strips, shape, *refs):
    index_ref = refs[0]
    heads = refs[1:1 + strips]
    places_ref, grads_ref = refs[1 + strips:3 + strips]
    outs = refs[3 + strips:3 + strips + inner]
    spread_ref, total_ref = refs[-2:]
    count, slots, near, _, part, width = shape
    length = slots * part
    step = pl.program_id(0)
    head = jnp.concatenate([ref[...] for ref in heads], axis=1)
    token = lax.broadcasted_iota(jnp.int32, (length, head.shape[0]), 0)
    for k in range(docs):
        spread = jnp.where(token == places_ref[pl.ds(k, 1), :], grads_ref[pl.ds(k, 1), :], 0.0)
        spread_ref[pl.ds(k * length, length), :] = spread.astype(jnp.bfloat16)
    term = jnp.dot(spread_ref[...], head, preferred_element_type=jnp.float32)

    @pl.when(step == 0)
    def _():
        total_ref[...] = term

    @pl.when(step > 0)
    def _():
        total_ref[...] += term

    @pl.when(step == pl.num_programs(0) - 1)
    def _():
        for q in range(inner):
            lane_y = lax.rem(index_ref[0] + q, inner)
            for i in range(count):
                for n in range(near):
                    lane = pl.multiple_of(((i * near + n) * inner + lane_y) * width, width)
                    for k in range(docs):
                        for s in range(slots):
                            piece = total_ref[pl.ds(k * length + s * part, part), pl.ds(lane, width)]
                            outs[q][i, s, n, k] = piece.astype(jnp.bfloat16)


def combine_kernel(inner, slots, index_ref, *refs):
    parts, outs = refs[:inner], refs[inner:]
    for i in range(parts[0].shape[0]):
        for s in range(slots):
            total = parts[0][i, s].astype(jnp.float32)
            for other in parts[1:]:
                total = total + other[i, s].astype(jnp.float32)
            outs[s][i] = total.astype(jnp.bfloat16)


def columns_kernel(groups, docs, index_ref, *refs):
    packed = refs[:groups]
    out_ref, turned_ref = refs[groups:]
    steps, _, columns = packed[0].shape
    count = groups * docs
    turned_ref[...] = jnp.zeros_like(turned_ref)
    for step in range(steps):
        for first in range(groups):

            @pl.when(index_ref[1] == first)
            def _():
                for g in range(groups):
                    place = (first + g) % groups * docs
                    turned_ref[place:place + docs, :columns] = packed[g][step, :docs]
                    turned_ref[count + place:count + place + docs, :columns] = packed[g][step, docs:2 * docs]

        turned = turned_ref[...].T
        out_ref[step * columns:(step + 1) * columns, :] = turned[:columns, :2 * count]


def sort_kernel(slots, near, outer, index_ref, *refs):
    mine, outs = refs[:slots], refs[slots:]
    block_z, seq = index_ref[2], index_ref[3]
    for ahead in range(outer):
        z = lax.rem(block_z + ahead, outer)
        slot = lax.rem(seq + slots - lax.div(z, near), slots)
        for s in range(slots):

            @pl.when(slot == s)
            def _():
                outs[ahead][...] = mine[s][:, lax.rem(z, near)]


def finish_kernel(counts, outer, index_ref, margin_ref, *refs):
    out_ref = refs[-1]
    docs = out_ref.shape[0]
    width = refs[0].shape[-1]
    c = 0
    for group, count in enumerate(counts):
        arrived = refs[group * outer:(group + 1) * outer]
        for i in range(count):
            for k in range(docs):
                total = arrived[0][i, k].astype(jnp.float32)
                for other in arrived[1:]:
                    total = total + other[i, k].astype(jnp.float32)
                out_ref[k, :, c * width:(c + 1) * width] = (total * margin_ref[k // 3]).astype(jnp.bfloat16)
            c += 1


def head_kernel(groups, docs, *refs):
    index_ref, margin_ref = refs[:2]
    rows = refs[2:2 + groups]
    columns_ref = refs[2 + groups]
    out_ref, token_ref, spread_ref = refs[-3:]
    chunks, tokens, width = rows[0].shape
    length = tokens // docs
    count = groups * docs

    @pl.when(pl.program_id(1) == 0)
    def _():
        token_ref[...] = jnp.zeros_like(token_ref)
        token = lax.broadcasted_iota(jnp.int32, (out_ref.shape[0], length), 1).astype(jnp.float32)
        for k in range(count):
            grads = columns_ref[:, k:k + 1] * margin_ref[k // 3]
            spread = jnp.where(token == columns_ref[:, count + k:count + k + 1], grads, 0.0)
            spread_ref[:, k * length:(k + 1) * length] = spread.astype(jnp.bfloat16)

    for first in range(groups):

        @pl.when(index_ref[1] == first)
        def _():
            total = None
            for g in range(groups):
                ref = rows[(g - first) % groups]
                features = jnp.concatenate([ref[c] for c in range(chunks)], axis=1)
                term = jnp.dot(
                    spread_ref[:, g * tokens:(g + 1) * tokens], features, preferred_element_type=jnp.float32
                )
                total = term if total is None else total + term
            out_ref[...] = total


def on_device(axes, hidden_states, head_weight, owner_pos, token_ids, teacher_margin):
    groups, slots, blocks = axes
    docs, part, block_width = hidden_states.shape
    depth, terms = head_weight.shape
    triples = teacher_margin.shape[0]
    inner = 2 if blocks % 2 == 0 else 1
    outer = blocks // inner
    near = outer // slots
    chunks = max(1, block_width // LANES)
    width = block_width // chunks
    length = slots * part
    tokens = docs * length
    columns = divisor(terms, 2048)
    steps = terms // columns
    strips = near * inner

    group = lax.axis_index("dp")
    seq = lax.axis_index("seq")
    block = lax.axis_index("vocab")
    block_y = lax.rem(block, inner)
    block_z = lax.div(block, inner)
    index = jnp.stack([block_y, group, block_z, seq]).astype(jnp.int32)

    def across_y(value, shift):
        perm = [(z * inner + y, z * inner + (y + shift) % inner) for z in range(outer) for y in range(inner)]
        return lax.ppermute(value, "vocab", perm)

    order = [0] + list(range(1, outer, 2)) + [z for z in range(outer - 1, 0, -1) if z % 2 == 0]

    def around_ring(value, steps_on):
        perm = [
            (order[p] * inner + y, order[(p + steps_on) % outer] * inner + y)
            for p in range(outer)
            for y in range(inner)
        ]
        return lax.ppermute(value, "vocab", perm)

    def across_z(value, shift):
        perm = [(z * inner + y, (z + shift) % outer * inner + y) for z in range(outer) for y in range(inner)]
        return lax.ppermute(value, "vocab", perm)

    def other_groups(value):
        return [value] + [lax.ppermute(value, "dp", shift_perm(groups, -g)) for g in range(1, groups)]

    def in_group_order(values):
        doubled = jnp.stack(values + values)
        return lax.dynamic_slice_in_dim(doubled, lax.rem(groups - group, groups), groups, axis=0)

    def blocked(value):
        return value.reshape(docs, steps, columns).transpose(1, 0, 2)

    head_rows = head_weight.T
    strip_specs = lambda c: [
        pl.BlockSpec((columns, width), functools.partial(lambda lane, v: (v, lane), strip * chunks + c))
        for strip in range(strips)
    ]
    row_spec = pl.BlockSpec((pl.squeezed, docs, columns), lambda v: (v, 0, 0))
    piece_shape = (slots, near, docs, part, width)
    piece_spec = pl.BlockSpec(piece_shape, lambda v: (0, 0, 0, 0, 0))
    index_spec = pl.BlockSpec(memory_space=pltpu.SMEM)
    vmem_spec = pl.BlockSpec(memory_space=pltpu.VMEM)
    any_spec = pl.BlockSpec(memory_space=pl.ANY)

    def cost(flops, transferred):
        return pl.CostEstimate(flops=int(flops), bytes_accessed=int(transferred), transcendentals=0)

    owner_blocks = blocked(owner_pos)
    places = lax.rem(owner_blocks + (length - seq * part), length)
    own_lengths = jnp.sum((token_ids != 0).astype(jnp.int32), axis=1, keepdims=True)
    lengths = own_lengths
    for s in range(1, slots):
        lengths = lengths + lax.ppermute(own_lengths, "seq", shift_perm(slots, s))
    validity = (owner_blocks < lengths[None]).astype(jnp.float32)

    def run(kernel, name, operands, specs, shapes, out_specs=None, waits=(), flops=0, aliases={}, scratch=(), grid=(), limit=VMEM_BYTES):
        waits = [value for value in waits if value is not None]
        return pl.pallas_call(
            waiting(kernel, len(waits)),
            grid=grid,
            in_specs=[index_spec] + [any_spec] * len(waits) + specs,
            out_specs=out_specs or [vmem_spec] * len(shapes),
            out_shape=shapes,
            scratch_shapes=list(scratch),
            input_output_aliases={1 + len(waits) + i: o for i, o in aliases.items()},
            compiler_params=pltpu.CompilerParams(vmem_limit_bytes=limit),
            cost_estimate=cost(flops, flops // 64),
            name=name,
        )(index, *waits, *operands)

    bf16 = lambda *shape: jax.ShapeDtypeStruct(shape, jnp.bfloat16)
    moved_shape = bf16(near, docs, part, width)
    sliced = [hidden_states[:, :, c * width:(c + 1) * width] for c in range(chunks)]
    last = chunks - 1
    gathered_chunks = []
    others = []
    logit_parts = []
    features = None

    def add_logits(c, waits):
        nonlocal features
        previous = [] if features is None else [features]
        chunk_logits, features = run(
            functools.partial(logits_kernel, docs, inner, strips),
            "pooled_logits",
            [gathered_chunks[c], others[c]][:inner] + [head_rows] * strips + [places, *previous],
            [piece_spec] * inner + strip_specs(c) + [row_spec] + [any_spec] * len(previous),
            [
                jax.ShapeDtypeStruct((steps, docs, columns), jnp.float32),
                bf16(chunks, tokens, strips * width),
            ],
            out_specs=[
                row_spec,
                pl.BlockSpec(
                    (pl.squeezed, tokens, strips * width), functools.partial(lambda c, v: (c, 0, 0), c)
                ),
            ],
            waits=waits,
            flops=2 * tokens * strips * width * terms,
            aliases={inner + strips + 1: 1} if previous else {},
            grid=(steps,),
        )
        logit_parts.append(chunk_logits)

    first_step = None
    for c in range(chunks):
        own = sliced[c]
        if c > 0:
            (own,) = run(
                copy_kernel, "feature_chunk", [own], [vmem_spec], [bf16(docs, part, width)], waits=[first_step]
            )
        held = [own]
        for back in range(1, outer):
            held.append(around_ring(own, back) if c == 0 else around_ring(held[-1], 1))
        first_step = held[min(1, outer - 1)]
        mine, *sends = run(
            functools.partial(pick_kernel, slots, near, outer),
            "pick_halves",
            held,
            [vmem_spec] * outer,
            [moved_shape] * slots,
            waits=[gathered_chunks[c - 1] if c > 0 else None],
        )
        arrived = [lax.ppermute(sends[s - 1], "seq", shift_perm(slots, -s)) for s in range(1, slots)]
        if c == last and c > 1:
            add_logits(0, [mine])
        (gathered,) = run(
            join_kernel,
            "join_tokens",
            [mine, *arrived],
            [vmem_spec] * slots,
            [bf16(*piece_shape)],
            waits=[others[c - 2] if c > 1 else None, logit_parts[0] if logit_parts else None],
        )
        gathered_chunks.append(gathered)
        others.append(across_y(gathered, -1) if inner > 1 else None)
    for c in range(len(logit_parts), chunks):
        add_logits(c, [validity, others[-2]] if c == 1 else [])

    logit_part = functools.reduce(jnp.add, logit_parts)
    logits = logit_part
    for s in range(1, slots):
        logits = logits + lax.ppermute(logit_part, "seq", shift_perm(slots, s))
    softened = jax.nn.softplus(logits)
    pooled = validity * jnp.log1p(softened)
    slopes = validity * jax.nn.sigmoid(logits) / (1.0 + softened)
    view = pooled.reshape(steps, triples, 3, columns)
    query, positive, negative = view[:, :, 0], view[:, :, 1], view[:, :, 2]
    unscaled = jnp.stack([positive - negative, query, -query], axis=2).reshape(logits.shape) * slopes
    unscaled = unscaled.astype(jnp.bfloat16)
    unscaled = unscaled.astype(jnp.float32)
    scores = jnp.sum(query * positive, axis=(0, 2)) - jnp.sum(query * negative, axis=(0, 2))
    paired = blocks & (blocks - 1) == 0
    distance = 1

    def add_distance(value, distance):
        return value + lax.ppermute(value, "vocab", [(i, i ^ distance) for i in range(blocks)])

    if paired and blocks > 1:
        scores = add_distance(scores, distance)
        distance *= 2
    score_row = jnp.pad(jnp.concatenate([scores, teacher_margin]), (0, columns - 2 * triples))
    packed = jnp.concatenate(
        [unscaled, places.astype(jnp.float32), jnp.broadcast_to(score_row, (steps, 1, columns))], axis=1
    )
    packed_all = other_groups(packed)
    scores = in_group_order([scores] + [value[0, 2 * docs, :triples] for value in packed_all[1:]])
    teacher = in_group_order([teacher_margin] + [value[0, 2 * docs, triples:2 * triples] for value in packed_all[1:]])
    if paired:
        while distance < blocks:
            scores = add_distance(scores, distance)
            distance *= 2
    else:
        scores = lax.psum(scores, "vocab")
    margin_all = ((scores - teacher) / (triples * groups)).reshape(-1)
    margin = lax.dynamic_slice(margin_all, (group * triples,), (triples,))
    (head_columns,) = run(
        functools.partial(columns_kernel, groups, docs),
        "turn_gradients",
        packed_all,
        [vmem_spec] * groups,
        [jax.ShapeDtypeStruct((terms, 2 * groups * docs), jnp.float32)],
        scratch=[pltpu.VMEM((-(-2 * groups * docs // 8) * 8, -(-columns // LANES) * LANES), jnp.float32)],
    )
    features_all = other_groups(features)

    head_terms = divisor(terms, 800)
    ranges = terms // head_terms
    next_range = 0
    grad_head = token = None

    def run_head(count, *waits):
        nonlocal grad_head, token, next_range
        if count == 0:
            return
        previous = [] if grad_head is None else [grad_head]
        start = next_range
        term_spec = pl.BlockSpec((head_terms, 2 * groups * docs), lambda r, d: (start + r, 0))
        grad_head, token = run(
            functools.partial(head_kernel, groups, docs),
            "head_terms",
            [margin_all, *features_all, head_columns, *previous],
            [index_spec]
            + [pl.BlockSpec((chunks, tokens, width), lambda r, d: (0, 0, d))] * groups
            + [term_spec]
            + [any_spec] * len(previous),
            [jax.ShapeDtypeStruct((terms, depth), jnp.float32), jax.ShapeDtypeStruct((8, LANES), jnp.float32)],
            out_specs=[
                pl.BlockSpec((head_terms, block_width), lambda r, d: (start + r, d)),
                pl.BlockSpec((8, LANES), lambda r, d: (0, 0)),
            ],
            waits=waits,
            flops=count * 2 * groups * tokens * head_terms * depth // 4,
            aliases={2 + groups: 0} if previous else {},
            scratch=[pltpu.VMEM((head_terms, groups * tokens), jnp.bfloat16)],
            grid=(count, strips),
            limit=HEAD_VMEM_BYTES,
        )
        next_range += count

    half = -(-chunks // 2)
    chunk_groups = [members for members in (range(half), range(half, chunks)) if members]
    pairs = []
    for members in chunk_groups:
        pair_shape = (len(members), *piece_shape)
        lanes = len(members) * strips * width
        sums = run(
            functools.partial(hidden_kernel, docs, inner, len(members) * strips, pair_shape),
            "hidden_terms",
            [head_rows] * (len(members) * strips) + [places, unscaled],
            [spec for c in members for spec in strip_specs(c)] + [row_spec, row_spec],
            [bf16(*pair_shape)] * inner,
            out_specs=[pl.BlockSpec(pair_shape, lambda v: (0,) * 6)] * inner,
            waits=[packed] if pairs else [],
            flops=2 * tokens * lanes * terms // 4,
            scratch=[pltpu.VMEM((tokens, columns), jnp.bfloat16), pltpu.VMEM((tokens, lanes), jnp.float32)],
            grid=(steps,),
        )
        pairs.append([sums[0]] + [across_y(sums[q], q) for q in range(1, inner)])

    share = ranges // 5
    mine_all = []
    arrived_all = []

    def add_blocks(pair, *waits):
        count = pair[0].shape[0]
        mine = run(
            functools.partial(combine_kernel, inner, slots),
            "add_blocks",
            pair,
            [vmem_spec] * inner,
            [bf16(count, near, docs, part, width)] * slots,
            waits=waits,
        )
        mine_all.append([mine[0]] + [lax.ppermute(mine[s], "seq", shift_perm(slots, s)) for s in range(1, slots)])

    def sort_pieces(mine, *waits):
        pieces = run(
            functools.partial(sort_kernel, slots, near, outer),
            "sort_pieces",
            mine,
            [vmem_spec] * slots,
            [bf16(mine[0].shape[0], docs, part, width)] * outer,
            waits=waits,
        )
        arrived_all.append([pieces[0]] + [across_z(pieces[ahead], ahead) for ahead in range(1, outer)])

    add_blocks(pairs[0])
    run_head(2 * share, mine_all[0][0], pairs[-1][0])
    sort_pieces(mine_all[0], token)
    if len(pairs) > 1:
        add_blocks(pairs[1], arrived_all[0][0])
        run_head(share, arrived_all[0][0], mine_all[1][0])
        sort_pieces(mine_all[1], token)
    run_head(ranges - next_range, arrived_all[-1][0])
    (grad_hidden,) = run(
        functools.partial(finish_kernel, [len(members) for members in chunk_groups], outer),
        "scale_hidden",
        [margin] + [value for arrived in arrived_all for value in arrived],
        [index_spec] + [vmem_spec] * (len(pairs) * outer),
        [bf16(docs, part, block_width)],
        waits=[token],
    )
    return (grad_head.T, grad_hidden)


def solution(mesh):
    axes = (mesh.shape["dp"], mesh.shape["seq"], mesh.shape["vocab"])
    return jax.shard_map(
        functools.partial(on_device, axes),
        mesh=mesh,
        in_specs=(
            P("dp", "seq", "vocab"),
            P("seq", "vocab"),
            P("dp", "vocab"),
            P("dp", "seq"),
            P("dp"),
        ),
        out_specs=(P("seq", "vocab"), P("dp", "seq", "vocab")),
        check_vma=False,
    )
```
